32 devices in a mesh: grp: 4 (over y, x), tile: 8 (over z, core).
Axes of the slice: x: 2, y: 2, z: 4, core: 2. Of those that a mesh axis runs over, the one named last changes fastest.
Arguments:
- latent: bfloat16 [8, 16, 16, 512], P(None, 'grp', 'tile'), may hold values from -36 to 36
- coarse_filters: bfloat16 [3, 3, 3, 512, 512], P(None, None, None, None, 'grp'), may hold values from -0.0546875 to 0.0546875
- mid_filters: bfloat16 [3, 3, 3, 256, 256], P(None, None, None, None, 'tile'), may hold values from -0.078125 to 0.078125
- fine_filters: bfloat16 [3, 3, 3, 128, 128], replicated, may hold values from -0.109375 to 0.109375
- coarse_proj: bfloat16 [512, 256], replicated, may hold values from -0.25 to 0.25
- mid_proj: bfloat16 [256, 128], replicated, may hold values from -0.375 to 0.375
Outputs:
- frames_out: bfloat16 [8, 64, 64, 128], P(None, 'grp', 'tile')
The draws below stay inside these ranges and needn't reach their ends.
All inputs are finite; a program needn't handle non-finite values.
Results may differ from the reference program's by a relative error of at most 0.018.
Values may be sent and summed in bfloat16 or wider, within the bound.
No kernel may reach another device: no remote copies, remote signals or barrier semaphores. Data moves between devices by JAX's collectives and lax.ppermute only.
A program may use at most 128 MiB of HBM per device.

```python
import math
import jax
import jax.numpy as jnp
from jax import lax

C0 = 512
C1 = 256
C2 = 128
FRAMES = 8
H0 = 16
W0 = 16


def draw_latent(key, part):
    keys = jax.random.split(key, 3)
    shape = (FRAMES, H0, W0, C0)
    cell_scale = jnp.exp(jax.random.uniform(keys[0], (FRAMES, H0, W0, 1), jnp.float32, math.log(0.3), math.log(3.0)))
    chan_scale = jnp.exp(jax.random.uniform(keys[1], (1, 1, 1, C0), jnp.float32, math.log(0.3), math.log(3.0)))
    base = jax.random.normal(keys[2], shape, jnp.float32)
    base = jnp.clip(base, -4.0, 4.0)
    return (base * cell_scale * chan_scale).astype(jnp.bfloat16)


def block_scale(own_key, extent, pieces, least, largest):
    level, own = 1.0, jax.random.fold_in(own_key, 6)
    for axis_at, parts in pieces:
        draws = jnp.exp(jax.random.uniform(jax.random.fold_in(own, axis_at), (parts,), jnp.float32, least / len(pieces), largest / len(pieces)))
        level = level * jnp.repeat(draws, extent[axis_at] // parts).reshape([-1 if axis == axis_at else 1 for axis in range(len(extent))])
    return level


def gaussian(stream_key, extent, deviation, limit, shards=(), dtype=jnp.bfloat16):
    drawn = deviation * jax.random.normal(stream_key, extent, jnp.float32)
    if shards:
        drawn = drawn * block_scale(stream_key, extent, shards, -0.22, 0.18)
    return jnp.clip(drawn, -limit, limit).astype(dtype)


def setup_inputs(seed: int = 0) -> dict:
    streams_of = jax.random.split(jax.random.key(seed), 7)
    return {
        "latent": draw_latent(jax.random.fold_in(streams_of[6], 71), 0),
        "coarse_filters": gaussian(streams_of[1], (3, 3, 3, C0, C0), (27 * C0) ** -0.5, 0.0546875, ((4, 4),)),
        "mid_filters": gaussian(streams_of[2], (3, 3, 3, C1, C1), (27 * C1) ** -0.5, 0.078125, ((4, 8),)),
        "fine_filters": gaussian(streams_of[3], (3, 3, 3, C2, C2), (27 * C2) ** -0.5, 0.109375),
        "coarse_proj": gaussian(streams_of[4], (C0, C1), C0 ** -0.5, 0.25),
        "mid_proj": gaussian(streams_of[5], (C1, C2), C1 ** -0.5, 0.375),
    }


def activate(values):
    widened = values.astype(jnp.float32)
    scaled = widened * lax.rsqrt(lax.optimization_barrier(jnp.mean(widened * widened, axis=-1, keepdims=True)) + 1e-06)
    return jax.nn.silu(scaled).astype(jnp.bfloat16)

def double_size(values):
    return jnp.repeat(jnp.repeat(values, 2, axis=1), 2, axis=2)

def causal_conv(values, filters):
    result = lax.conv_general_dilated(values[None], filters, window_strides=(1, 1, 1), padding=((2, 0), (1, 1), (1, 1)), dimension_numbers=('NDHWC', 'DHWIO', 'NDHWC'), preferred_element_type=jnp.float32)
    return result[0]

def reference(latent, coarse_filters, mid_filters, fine_filters, coarse_proj, mid_proj):
    coarse_out = causal_conv(activate(latent), coarse_filters).astype(jnp.bfloat16)
    level_zero = (latent.astype(jnp.float32) + coarse_out.astype(jnp.float32)).astype(jnp.bfloat16)
    reduced = jnp.dot(level_zero, coarse_proj, preferred_element_type=jnp.float32).astype(jnp.bfloat16)
    mid_act = double_size(activate(reduced))
    mid_out = (double_size(reduced).astype(jnp.float32) + causal_conv(mid_act, mid_filters)).astype(jnp.bfloat16)
    fine_low = jnp.dot(mid_out, mid_proj, preferred_element_type=jnp.float32).astype(jnp.bfloat16)
    fine_act = double_size(activate(fine_low))
    return (double_size(fine_low).astype(jnp.float32) + causal_conv(fine_act, fine_filters)).astype(jnp.bfloat16)
```

```python
import functools

import jax
import jax.numpy as jnp
from jax import lax
from jax.experimental import pallas as pl
from jax.experimental.pallas import tpu as pltpu
from jax.sharding import PartitionSpec as P

VMEM = pl.BlockSpec(memory_space=pltpu.VMEM)
F32 = jnp.float32
BF16 = jnp.bfloat16


def call(kernel, outs, scratch, flops, nbytes, *args):
    return pl.pallas_call(
        kernel,
        out_shape=outs,
        in_specs=[VMEM] * len(args),
        out_specs=jax.tree.map(lambda _: VMEM, outs),
        scratch_shapes=scratch,
        compiler_params=pltpu.CompilerParams(vmem_limit_bytes=40 << 20),
        cost_estimate=pl.CostEstimate(flops=flops, bytes_accessed=nbytes, transcendentals=0),
    )(*args)


def dot(left, right):
    return jnp.dot(left, right, preferred_element_type=F32)


def activate(values):
    scaled = values * lax.rsqrt(jnp.mean(values * values, axis=-1, keepdims=True) + 1e-06)
    return scaled / (1.0 + jnp.exp(-scaled))


def delayed(values, steps):
    if steps == 0:
        return values
    axis = values.ndim - 2
    frame = lax.broadcasted_iota(jnp.int32, values.shape, axis)
    return jnp.where(frame >= steps, pltpu.roll(values, steps, axis), 0.0)


def coarse_kernel(groups, *refs):
    pieces, (filters, proj, part, straight, shifted) = refs[:groups], refs[groups:]
    rows, cols, frames, depth = pieces[0].shape
    width = filters.shape[4]
    height = groups * rows
    me = lax.axis_index("grp")
    edge = jnp.zeros((1, cols * frames, depth), BF16)
    for step in range(3):
        shifted[step, 0:1] = edge
        shifted[step, height + 1 : height + 2] = edge
    for k in range(groups):
        at = (me ^ k) * rows
        raw = pieces[k][...]
        flat = raw.reshape(rows * cols * frames, depth)
        direct = dot(flat, proj[...]).reshape(rows, cols, frames, proj.shape[1])
        for col in range(cols):
            straight[col, pl.ds(at, rows)] = direct[:, col]
        act = activate(raw.astype(F32))
        for step in range(3):
            moved = delayed(act, 2 - step).reshape(rows, cols * frames, depth)
            shifted[step, pl.ds(at + 1, rows)] = moved.astype(BF16)
    joined = width % 128 == 0
    totals = [None] * (1 if joined else 3)
    for step in range(3):
        for row in range(3):
            left = shifted[step, row : row + height].reshape(height * cols * frames, depth)
            taps = [filters[step, row, col] for col in range(3)]
            if joined:
                taps = [jnp.concatenate(taps, axis=1)]
            for n, tap in enumerate(taps):
                term = dot(left, tap)
                totals[n] = term if totals[n] is None else totals[n] + term
    if joined:
        totals = [totals[0][:, n * width : (n + 1) * width] for n in range(3)]
    totals = [total.reshape(height, cols, frames, width) for total in totals]
    for out in range(cols + 2):
        value = sum(
            totals[tap][:, out - 2 + tap] for tap in range(3) if 0 <= out - 2 + tap < cols
        )
        part[out] = value.reshape(height * frames, width).astype(BF16)


def project_kernel(groups, *refs):
    parts, (proj, straight, own, even_out, odd_out) = refs[:groups], refs[groups:]
    extent, cells, width = parts[0].shape
    outputs = proj.shape[2]
    total = None
    for k in range(groups):
        term = dot(parts[k][...].reshape(extent * cells, width), proj[k])
        total = term if total is None else total + term
    total = total.reshape(extent, cells, outputs)
    cols = extent - 2
    middle = total[1 : cols + 1] + straight[...].reshape(cols, cells, outputs)
    own[0] = total[0]
    own[1 : cols + 1] = middle
    own[cols + 1] = total[cols + 1]
    left = jnp.stack([total[0], middle[0]])
    right = jnp.stack([middle[cols - 1], total[cols + 1]])
    odd = lax.axis_index("tile") % 2 == 1
    even_out[...] = jnp.where(odd, left, right).astype(BF16)
    odd_out[...] = jnp.where(odd, right, left).astype(BF16)


def middle_kernel(groups, rows, frames, own, even_in, odd_in, filters, *refs):
    outs, (block, acts, acts_odd, kept, sums) = refs[:groups], refs[groups:]
    extent, cells, depth = own.shape
    cols = extent - 2
    height = cells // frames
    me = lax.axis_index("grp")
    tile = lax.axis_index("tile")
    odd = tile % 2 == 1
    even_got = even_in[...].astype(F32)
    odd_got = odd_in[...].astype(F32)
    from_left = jnp.where(odd, even_got, odd_got)
    from_right = jnp.where(odd, odd_got, even_got)
    values = []
    for col in range(extent):
        value = own[col]
        if col < 2:
            value = value + from_left[col]
        if col >= cols:
            value = value + from_right[col - cols]
        if col == 0:
            value = jnp.where(tile == 0, 0.0, value)
        if col == extent - 1:
            value = jnp.where(tile == lax.axis_size("tile") - 1, 0.0, value)
        values.append(value.astype(BF16).astype(F32).reshape(height, frames, depth))
    nothing = jnp.zeros((1, frames, depth), F32)
    for col in range(extent):
        kept[col, 0:1] = nothing
        kept[col, 1 : height + 1] = values[col]
        kept[col, height + 1 : height + 2] = nothing
        act = activate(values[col])
        for step in range(3):
            moved = delayed(act, 2 - step)
            framed = jnp.concatenate([nothing, moved, nothing], axis=0)
            acts[step, col] = framed.reshape(cells + 2 * frames, depth).astype(BF16)
            acts_odd[step, col] = moved.reshape(cells, depth).astype(BF16)
    block[...] = (
        kept[:, pl.ds(me * rows, rows + 2)]
        .reshape(extent, (rows + 2) * frames, depth)
        .astype(BF16)
    )
    pairs = extent - 1
    total = None
    for step in range(3):
        for row in range(3):
            for side in range(2):
                if row == 1:
                    left = acts_odd[step, side : side + pairs]
                else:
                    first = row * frames
                    left = acts[step, side : side + pairs, first : first + cells]
                term = dot(left.reshape(pairs * cells, depth), filters[step, row, side])
                total = term if total is None else total + term
    lanes = total.shape[1]
    total = total.reshape(pairs, height, frames, lanes)
    empty = jnp.zeros((pairs, 1, frames, lanes), F32)
    sums[:, 0:1] = empty
    sums[:, 1 : height + 1] = total
    sums[:, height + 1 : height + 2] = empty
    for k in range(groups):
        chunk = sums[:, pl.ds((me ^ k) * rows, rows + 2)]
        outs[k][...] = chunk.reshape(pairs, (rows + 2) * frames, lanes).astype(BF16)


def fine_kernel(groups, frames, *refs):
    chunks = refs[:groups]
    block, spread, proj, filters, out, acts, acts_odd, lows = refs[groups:]
    pairs, cells, lanes = chunks[0].shape
    extent = block.shape[0]
    rows = cells // frames - 2
    width = proj.shape[1]
    tall, broad = 2 * rows, 2 * (extent - 2)
    me, last_me = lax.axis_index("grp"), lax.axis_size("grp") - 1
    tile, last_tile = lax.axis_index("tile"), lax.axis_size("tile") - 1
    total = None
    for k in range(groups):
        term = dot(chunks[k][...].reshape(pairs * cells, lanes), spread[k])
        total = term if total is None else total + term
    total = total.reshape(pairs, rows + 2, frames, 4 * width)
    base = dot(block[...].reshape(extent * cells, block.shape[2]), proj[...])
    base = base.reshape(extent, rows + 2, frames, width)
    nothing = jnp.zeros((1, frames, width), F32)
    for col in range(broad + 2):
        pair, side = divmod(col, 2)
        upper, lower = [
            total[pair, :, :, (2 * p + side) * width : (2 * p + side + 1) * width]
            + base[pair + side]
            for p in range(2)
        ]
        woven = jnp.stack([lower[: rows + 1], upper[1:]], axis=1)
        value = woven.reshape(tall + 2, frames, width).astype(BF16).astype(F32)
        if col == 0:
            value = jnp.where(tile == 0, 0.0, value)
        if col == broad + 1:
            value = jnp.where(tile == last_tile, 0.0, value)
        top = jnp.where(me == 0, 0.0, value[0:1])
        bottom = jnp.where(me == last_me, 0.0, value[tall + 1 : tall + 2])
        value = jnp.concatenate([top, value[1 : tall + 1], bottom], axis=0)
        lows[col] = value[1 : tall + 1]
        act = activate(value)
        for step in range(3):
            moved = delayed(act, 2 - step)
            acts[step, col] = moved.reshape((tall + 2) * frames, width).astype(BF16)
            acts_odd[step, col] = (
                moved[1 : tall + 1].reshape(tall * frames, width).astype(BF16)
            )
    span = broad + 1
    strip = tall * frames
    for p in range(2):
        sums = None
        for step in range(3):
            for near in range(2):
                row = p + near
                if row == 1:
                    pick = [acts_odd[step, side : side + span] for side in range(2)]
                else:
                    first = row * frames
                    pick = [
                        acts[step, side : side + span, first : first + strip]
                        for side in range(2)
                    ]
                left = jnp.concatenate([v.reshape(span * strip, width) for v in pick], axis=1)
                term = dot(left, filters[step, p, near])
                sums = term if sums is None else sums + term
        sums = sums.reshape(span, tall, frames, 2 * width)
        fields = []
        for col in range(2 * broad):
            pair, side = divmod(col + 1, 2)
            low = lows[pair + side]
            fields.append(sums[pair, :, :, side * width : (side + 1) * width] + low)
        field = jnp.stack(fields, axis=1)
        for row in range(tall):
            out[:, 2 * row + p] = jnp.swapaxes(field[row], 0, 1).astype(BF16)


def fold_middle_kernel(pieces, out):
    parts, n, depth = pieces.shape[0], pieces.shape[4], pieces.shape[5]

    def per_step(step, carry):
        taps = [
            [
                pieces[:, step, row, col].astype(F32).reshape(parts * n, depth)
                for col in range(3)
            ]
            for row in range(3)
        ]
        nothing = jnp.zeros((parts * n, depth), F32)
        for side in range(2):
            narrow = [
                [taps[r][0] + taps[r][1] if side == 0 else taps[r][2],
                 taps[r][0] if side == 0 else taps[r][1] + taps[r][2]]
                for r in range(3)
            ]
            for row in range(3):
                blocks = []
                for p in range(2):
                    for q in range(2):
                        if row == 1:
                            value = narrow[1][q] + narrow[2 if p == 0 else 0][q]
                        elif row == 0:
                            value = narrow[0][q] if p == 0 else nothing
                        else:
                            value = nothing if p == 0 else narrow[2][q]
                        blocks.append(value)
                out[step, row, side] = jnp.concatenate(blocks, axis=0).T.astype(BF16)
        return carry

    lax.fori_loop(0, 3, per_step, 0)


def fold_fine_kernel(filters, out):
    def per_step(step, carry):
        taps = [[filters[step, r, c].astype(F32) for c in range(3)] for r in range(3)]
        for p in range(2):
            for near in range(2):
                if p == 0:
                    line = taps[0] if near == 0 else [x + y for x, y in zip(taps[1], taps[2])]
                else:
                    line = [x + y for x, y in zip(taps[0], taps[1])] if near == 0 else taps[2]
                first = jnp.concatenate([line[0] + line[1], line[0]], axis=1)
                second = jnp.concatenate([line[2], line[1] + line[2]], axis=1)
                out[step, p, near] = jnp.concatenate([first, second], axis=0).astype(BF16)
        return carry

    lax.fori_loop(0, 3, per_step, 0)


def reorder(values, index):
    size, rest = values.shape[0], values.shape[1:]
    bit = 1
    while bit < size:
        pairs = values.reshape(size // (2 * bit), 2, bit, *rest)
        pairs = jnp.where((index & bit) != 0, pairs[:, ::-1], pairs)
        values = pairs.reshape(size, *rest)
        bit *= 2
    return values


def exchange(values, axis, k):
    size = lax.axis_size(axis)
    return lax.ppermute(values, axis, [(i, i ^ k) for i in range(size)])


def body(latent, coarse_filters, mid_filters, fine_filters, coarse_proj, mid_proj):
    groups, tiles = lax.axis_size("grp"), lax.axis_size("tile")
    me, tile = lax.axis_index("grp"), lax.axis_index("tile")
    frames, rows, cols, depth0 = latent.shape
    depth1, depth2 = mid_proj.shape
    width0 = coarse_filters.shape[4]
    height = groups * rows
    cells = height * frames
    own_mid = mid_filters.shape[4]

    first = jnp.transpose(latent, (1, 2, 0, 3))
    pieces = [first] + [exchange(first, "grp", k) for k in range(1, groups)]

    mid_rows = jnp.transpose(mid_filters, (0, 1, 2, 4, 3))
    if own_mid % groups == 0 and (own_mid // groups) % 8 == 0:
        share = own_mid // groups
        mine = lax.dynamic_slice_in_dim(mid_rows, me * share, share, axis=3)[None]
        bit = 2
        while bit < tiles:
            mine = jnp.concatenate([mine, exchange(mine, "tile", bit)])
            bit *= 2
        mine = jnp.concatenate([mine, exchange(mine, "tile", 1)])
        table = mid_proj.reshape(tiles // 2, 2, groups, share, depth2).transpose(1, 0, 2, 3, 4)
        table = reorder(table, tile & 1)
        table = jnp.swapaxes(reorder(jnp.swapaxes(table, 0, 1), tile >> 1), 0, 1)
        table = table.transpose(2, 0, 1, 3, 4).reshape(groups, tiles * share, depth2)
    else:
        share = depth1 // groups
        every = lax.all_gather(mid_rows, "tile", axis=3, tiled=True)
        mine = lax.dynamic_slice_in_dim(every, me * share, share, axis=3)[None]
        table = mid_proj.reshape(groups, share, depth2)
    lanes = 4 * mine.shape[0] * mine.shape[4]
    table = reorder(table, me)
    spread = (
        jnp.eye(4, dtype=BF16)[None, :, None, :, None] * table[:, None, :, None, :]
    ).reshape(groups, lanes, 4 * depth2)
    proj = reorder(coarse_proj.reshape(groups, width0, depth1), me)

    fine_folded = call(
        fold_fine_kernel,
        jax.ShapeDtypeStruct((3, 2, 2, 2 * depth2, 2 * depth2), BF16),
        [],
        10**6,
        4 * 10**6,
        fine_filters,
    )
    mid_folded = call(
        fold_middle_kernel,
        jax.ShapeDtypeStruct((3, 3, 2, depth1, lanes), BF16),
        [],
        10**6,
        4 * 10**6,
        mine,
    )

    part, straight = call(
        functools.partial(coarse_kernel, groups),
        (
            jax.ShapeDtypeStruct((cols + 2, cells, width0), BF16),
            jax.ShapeDtypeStruct((cols, height, frames, depth1), F32),
        ),
        [pltpu.VMEM((3, height + 2, cols * frames, depth0), BF16)],
        2 * 27 * cells * cols * depth0 * width0,
        5 * 10**6,
        *pieces,
        coarse_filters,
        coarse_proj,
    )
    parts = [part] + [exchange(part, "grp", k) for k in range(1, groups)]
    own, even_out, odd_out = call(
        functools.partial(project_kernel, groups),
        (
            jax.ShapeDtypeStruct((cols + 2, cells, depth1), F32),
            jax.ShapeDtypeStruct((2, cells, depth1), BF16),
            jax.ShapeDtypeStruct((2, cells, depth1), BF16),
        ),
        [],
        2 * cells * (cols + 2) * depth0 * depth1,
        2 * 10**6,
        *parts,
        proj,
        straight,
    )
    odd_pairs = [(i, i + 1) for i in range(1, tiles - 1, 2)]
    even_in = exchange(even_out, "tile", 1)
    odd_in = lax.ppermute(odd_out, "tile", odd_pairs + [(j, i) for i, j in odd_pairs])
    local = (rows + 2) * frames
    *chunks, block = call(
        functools.partial(middle_kernel, groups, rows, frames),
        tuple(jax.ShapeDtypeStruct((cols + 1, local, lanes), BF16) for _ in range(groups))
        + (jax.ShapeDtypeStruct((cols + 2, local, depth1), BF16),),
        [
            pltpu.VMEM((3, cols + 2, cells + 2 * frames, depth1), BF16),
            pltpu.VMEM((3, cols + 2, cells, depth1), BF16),
            pltpu.VMEM((cols + 2, height + 2, frames, depth1), F32),
            pltpu.VMEM((cols + 1, height + 2, frames, lanes), F32),
        ],
        2 * 18 * (cols + 1) * cells * depth1 * lanes,
        5 * 10**6,
        own,
        even_in,
        odd_in,
        mid_folded,
    )
    chunks = [chunks[0]] + [exchange(chunks[k], "grp", k) for k in range(1, groups)]
    tall, broad = 2 * rows, 2 * cols
    return call(
        functools.partial(fine_kernel, groups, frames),
        jax.ShapeDtypeStruct((frames, 2 * tall, 2 * broad, depth2), BF16),
        [
            pltpu.VMEM((3, broad + 2, (tall + 2) * frames, depth2), BF16),
            pltpu.VMEM((3, broad + 2, tall * frames, depth2), BF16),
            pltpu.VMEM((broad + 2, tall, frames, depth2), F32),
        ],
        2 * 24 * (broad + 1) * tall * frames * depth2 * 2 * depth2,
        3 * 10**6,
        *chunks,
        block,
        spread,
        mid_proj,
        fine_folded,
    )


def solution(mesh):
    in_specs = (
        P(None, "grp", "tile", None),
        P(None, None, None, None, "grp"),
        P(None, None, None, None, "tile"),
        P(),
        P(),
        P(),
    )
    out_specs = P(None, "grp", "tile", None)
    return jax.shard_map(body, mesh=mesh, in_specs=in_specs, out_specs=out_specs, check_vma=False)
```

```python
import functools

import jax
import jax.numpy as jnp
from jax import lax
from jax.experimental import pallas as pl
from jax.experimental.pallas import tpu as pltpu
from jax.sharding import PartitionSpec as P

VMEM = pl.BlockSpec(memory_space=pltpu.VMEM)
FAR = pl.BlockSpec(memory_space=pltpu.HBM)
F32 = jnp.float32
BF16 = jnp.bfloat16


def call(kernel, outs, scratch, flops, nbytes, *args, stay=()):
    args = [
        pltpu.with_memory_space_constraint(arg, pltpu.HBM) if n in stay else arg
        for n, arg in enumerate(args)
    ]
    return pl.pallas_call(
        kernel,
        out_shape=outs,
        in_specs=[FAR if n in stay else VMEM for n in range(len(args))],
        out_specs=jax.tree.map(lambda _: VMEM, outs),
        scratch_shapes=scratch,
        compiler_params=pltpu.CompilerParams(vmem_limit_bytes=40 << 20),
        cost_estimate=pl.CostEstimate(flops=flops, bytes_accessed=nbytes, transcendentals=0),
    )(*args)


def dot(left, right):
    return jnp.dot(left, right, preferred_element_type=F32)


def activate(values):
    scaled = values * lax.rsqrt(jnp.mean(values * values, axis=-1, keepdims=True) + 1e-06)
    return scaled / (1.0 + jnp.exp(-scaled))


def delayed(values, steps):
    if steps == 0:
        return values
    axis = values.ndim - 2
    frame = lax.broadcasted_iota(jnp.int32, values.shape, axis)
    return jnp.where(frame >= steps, pltpu.roll(values, steps, axis), 0.0)


def coarse_kernel(groups, *refs):
    pieces, (filters, part, shifted) = refs[:groups], refs[groups:]
    rows, cols, frames, depth = pieces[0].shape
    width = filters.shape[4]
    height = groups * rows
    me = lax.axis_index("grp")
    edge = jnp.zeros((1, cols * frames, depth), BF16)
    for step in range(3):
        shifted[step, 0:1] = edge
        shifted[step, height + 1 : height + 2] = edge
    for k in range(groups):
        at = (me ^ k) * rows
        raw = pieces[k][...]
        act = activate(raw.astype(F32))
        for step in range(3):
            moved = delayed(act, 2 - step).reshape(rows, cols * frames, depth)
            shifted[step, pl.ds(at + 1, rows)] = moved.astype(BF16)
    joined = width % 128 == 0
    totals = [None] * (1 if joined else 3)
    for step in range(3):
        for row in range(3):
            left = shifted[step, row : row + height].reshape(height * cols * frames, depth)
            taps = [filters[step, row, col] for col in range(3)]
            if joined:
                taps = [jnp.concatenate(taps, axis=1)]
            for n, tap in enumerate(taps):
                term = dot(left, tap)
                totals[n] = term if totals[n] is None else totals[n] + term
    if joined:
        totals = [totals[0][:, n * width : (n + 1) * width] for n in range(3)]
    totals = [total.reshape(height, cols, frames, width) for total in totals]
    for out in range(cols + 2):
        value = sum(
            totals[tap][:, out - 2 + tap] for tap in range(3) if 0 <= out - 2 + tap < cols
        )
        part[out] = value.reshape(height * frames, width).astype(BF16)


def straight_kernel(groups, *refs):
    pieces, (proj, straight) = refs[:groups], refs[groups:]
    rows, cols, frames, depth = pieces[0].shape
    me = lax.axis_index("grp")
    for k in range(groups):
        flat = pieces[k][...].reshape(rows * cols * frames, depth)
        direct = dot(flat, proj[...]).reshape(rows, cols, frames, proj.shape[1])
        for col in range(cols):
            straight[col, pl.ds((me ^ k) * rows, rows)] = direct[:, col]


def project_kernel(groups, *refs):
    parts, (proj, straight, own, even_out, odd_out) = refs[:groups], refs[groups:]
    extent, cells, width = parts[0].shape
    outputs = proj.shape[1]
    me = lax.axis_index("grp")
    total = None
    for k in range(groups):
        weights = proj[pl.ds(pl.multiple_of((me ^ k) * width, width), width)]
        term = dot(parts[k][...].reshape(extent * cells, width), weights)
        total = term if total is None else total + term
    total = total.reshape(extent, cells, outputs)
    cols = extent - 2
    middle = total[1 : cols + 1] + straight[...].reshape(cols, cells, outputs)
    own[0] = total[0]
    own[1 : cols + 1] = middle
    own[cols + 1] = total[cols + 1]
    left = jnp.stack([total[0], middle[0]])
    right = jnp.stack([middle[cols - 1], total[cols + 1]])
    odd = lax.axis_index("tile") % 2 == 1
    even_out[...] = jnp.where(odd, left, right).astype(BF16)
    odd_out[...] = jnp.where(odd, right, left).astype(BF16)


def middle_kernel(groups, rows, frames, own, even_in, odd_in, filters, *refs):
    outs, (block, acts, acts_odd, kept, sums) = refs[:groups], refs[groups:]
    extent, cells, depth = own.shape
    cols = extent - 2
    height = cells // frames
    me = lax.axis_index("grp")
    tile = lax.axis_index("tile")
    odd = tile % 2 == 1
    even_got = even_in[...].astype(F32)
    odd_got = odd_in[...].astype(F32)
    from_left = jnp.where(odd, even_got, odd_got)
    from_right = jnp.where(odd, odd_got, even_got)
    values = []
    for col in range(extent):
        value = own[col]
        if col < 2:
            value = value + from_left[col]
        if col >= cols:
            value = value + from_right[col - cols]
        if col == 0:
            value = jnp.where(tile == 0, 0.0, value)
        if col == extent - 1:
            value = jnp.where(tile == lax.axis_size("tile") - 1, 0.0, value)
        values.append(value.astype(BF16).astype(F32).reshape(height, frames, depth))
    nothing = jnp.zeros((1, frames, depth), F32)
    for col in range(extent):
        kept[col, 0:1] = nothing
        kept[col, 1 : height + 1] = values[col]
        kept[col, height + 1 : height + 2] = nothing
        act = activate(values[col])
        for step in range(3):
            moved = delayed(act, 2 - step)
            framed = jnp.concatenate([nothing, moved, nothing], axis=0)
            acts[step, col] = framed.reshape(cells + 2 * frames, depth).astype(BF16)
            acts_odd[step, col] = moved.reshape(cells, depth).astype(BF16)
    block[...] = (
        kept[:, pl.ds(me * rows, rows + 2)]
        .reshape(extent, (rows + 2) * frames, depth)
        .astype(BF16)
    )
    pairs = extent - 1
    total = None
    for step in range(3):
        for row in range(3):
            for side in range(2):
                if row == 1:
                    left = acts_odd[step, side : side + pairs]
                else:
                    first = row * frames
                    left = acts[step, side : side + pairs, first : first + cells]
                term = dot(left.reshape(pairs * cells, depth), filters[step, row, side])
                total = term if total is None else total + term
    lanes = total.shape[1]
    total = total.reshape(pairs, height, frames, lanes)
    empty = jnp.zeros((pairs, 1, frames, lanes), F32)
    sums[:, 0:1] = empty
    sums[:, 1 : height + 1] = total
    sums[:, height + 1 : height + 2] = empty
    for k in range(groups):
        chunk = sums[:, pl.ds((me ^ k) * rows, rows + 2)]
        outs[k][...] = chunk.reshape(pairs, (rows + 2) * frames, lanes).astype(BF16)


def fine_kernel(groups, frames, *refs):
    chunks = refs[:groups]
    block, spread, proj, filters, out, acts, acts_odd, lows = refs[groups:]
    pairs, cells, lanes = chunks[0].shape
    extent = block.shape[0]
    rows = cells // frames - 2
    width = proj.shape[1]
    tall, broad = 2 * rows, 2 * (extent - 2)
    me, last_me = lax.axis_index("grp"), lax.axis_size("grp") - 1
    tile, last_tile = lax.axis_index("tile"), lax.axis_size("tile") - 1
    total = None
    for k in range(groups):
        term = dot(chunks[k][...].reshape(pairs * cells, lanes), spread[k])
        total = term if total is None else total + term
    total = total.reshape(pairs, rows + 2, frames, 4 * width)
    base = dot(block[...].reshape(extent * cells, block.shape[2]), proj[...])
    base = base.reshape(extent, rows + 2, frames, width)
    nothing = jnp.zeros((1, frames, width), F32)
    for col in range(broad + 2):
        pair, side = divmod(col, 2)
        upper, lower = [
            total[pair, :, :, (2 * p + side) * width : (2 * p + side + 1) * width]
            + base[pair + side]
            for p in range(2)
        ]
        woven = jnp.stack([lower[: rows + 1], upper[1:]], axis=1)
        value = woven.reshape(tall + 2, frames, width).astype(BF16).astype(F32)
        if col == 0:
            value = jnp.where(tile == 0, 0.0, value)
        if col == broad + 1:
            value = jnp.where(tile == last_tile, 0.0, value)
        top = jnp.where(me == 0, 0.0, value[0:1])
        bottom = jnp.where(me == last_me, 0.0, value[tall + 1 : tall + 2])
        value = jnp.concatenate([top, value[1 : tall + 1], bottom], axis=0)
        lows[col] = value[1 : tall + 1]
        act = activate(value)
        for step in range(3):
            moved = delayed(act, 2 - step)
            acts[step, col] = moved.reshape((tall + 2) * frames, width).astype(BF16)
            acts_odd[step, col] = (
                moved[1 : tall + 1].reshape(tall * frames, width).astype(BF16)
            )
    span = broad + 1
    strip = tall * frames
    for p in range(2):
        sums = None
        for step in range(3):
            for near in range(2):
                row = p + near
                if row == 1:
                    pick = [acts_odd[step, side : side + span] for side in range(2)]
                else:
                    first = row * frames
                    pick = [
                        acts[step, side : side + span, first : first + strip]
                        for side in range(2)
                    ]
                left = jnp.concatenate([v.reshape(span * strip, width) for v in pick], axis=1)
                term = dot(left, filters[step, p, near])
                sums = term if sums is None else sums + term
        sums = sums.reshape(span, tall, frames, 2 * width)
        fields = []
        for col in range(2 * broad):
            pair, side = divmod(col + 1, 2)
            low = lows[pair + side]
            fields.append(sums[pair, :, :, side * width : (side + 1) * width] + low)
        field = jnp.stack(fields, axis=1)
        for row in range(tall):
            out[:, 2 * row + p] = jnp.swapaxes(field[row], 0, 1).astype(BF16)


def fold_middle_kernel(pieces, out):
    parts, n, depth = pieces.shape[0], pieces.shape[4], pieces.shape[5]

    def per_step(step, carry):
        taps = [
            [
                pieces[:, step, row, col].astype(F32).reshape(parts * n, depth)
                for col in range(3)
            ]
            for row in range(3)
        ]
        nothing = jnp.zeros((parts * n, depth), F32)
        for side in range(2):
            narrow = [
                [taps[r][0] + taps[r][1] if side == 0 else taps[r][2],
                 taps[r][0] if side == 0 else taps[r][1] + taps[r][2]]
                for r in range(3)
            ]
            for row in range(3):
                blocks = []
                for p in range(2):
                    for q in range(2):
                        if row == 1:
                            value = narrow[1][q] + narrow[2 if p == 0 else 0][q]
                        elif row == 0:
                            value = narrow[0][q] if p == 0 else nothing
                        else:
                            value = nothing if p == 0 else narrow[2][q]
                        blocks.append(value)
                out[step, row, side] = jnp.concatenate(blocks, axis=0).T.astype(BF16)
        return carry

    lax.fori_loop(0, 3, per_step, 0)


def pick_kernel(groups, stored, out, filters, arrived):
    copy = pltpu.make_async_copy(stored, filters, arrived)
    copy.start()
    me = lax.axis_index("grp")
    share = out.shape[3]
    copy.wait()
    value = filters[:, :, :, 0:share].astype(F32)
    for k in range(1, groups):
        value = jnp.where(me == k, filters[:, :, :, k * share : (k + 1) * share].astype(F32), value)
    out[...] = value.astype(BF16)


def prepare_kernel(groups, parts, filters, proj, folded, spread, plain):
    def per_step(step, carry):
        taps = [[filters[step, r, c].astype(F32) for c in range(3)] for r in range(3)]
        for p in range(2):
            for near in range(2):
                if p == 0:
                    line = taps[0] if near == 0 else [x + y for x, y in zip(taps[1], taps[2])]
                else:
                    line = [x + y for x, y in zip(taps[0], taps[1])] if near == 0 else taps[2]
                first = jnp.concatenate([line[0] + line[1], line[0]], axis=1)
                second = jnp.concatenate([line[2], line[1] + line[2]], axis=1)
                folded[step, p, near] = jnp.concatenate([first, second], axis=0).astype(BF16)
        return carry

    lax.fori_loop(0, 3, per_step, 0)
    depth, width = proj.shape
    plain[...] = proj[...].astype(F32)
    me, tile = lax.axis_index("grp"), lax.axis_index("tile")
    share = depth // (groups * parts)
    spread[...] = jnp.zeros(spread.shape, BF16)
    for k in range(groups):
        lines = []
        for s in range(parts):
            if parts == 1:
                first = (me ^ k) * share
            else:
                source = tile ^ (s // (parts // 2)) ^ (2 * (s % (parts // 2)))
                first = (source * groups + (me ^ k)) * share
            lines.append(plain[pl.ds(pl.multiple_of(first, 8), share)])
        block = jnp.concatenate(lines, axis=0).astype(BF16)
        height = parts * share
        for phase in range(4):
            spread[
                k, phase * height : (phase + 1) * height, phase * width : (phase + 1) * width
            ] = block


def exchange(values, axis, k):
    size = lax.axis_size(axis)
    return lax.ppermute(values, axis, [(i, i ^ k) for i in range(size)])


def body(latent, coarse_filters, mid_filters, fine_filters, coarse_proj, mid_proj):
    groups, tiles = lax.axis_size("grp"), lax.axis_size("tile")
    me, tile = lax.axis_index("grp"), lax.axis_index("tile")
    frames, rows, cols, depth0 = latent.shape
    depth1, depth2 = mid_proj.shape
    width0 = coarse_filters.shape[4]
    height = groups * rows
    cells = height * frames
    own_mid = mid_filters.shape[4]

    divided = own_mid % groups == 0 and (own_mid // groups) % 8 == 0
    share, shares = (own_mid // groups, tiles) if divided else (depth1 // groups, 1)
    lanes = 4 * shares * share
    arrived = [exchange(latent, "grp", k) for k in range(1, groups)]
    arrived = lax.optimization_barrier(arrived)
    pieces = [jnp.transpose(piece, (1, 2, 0, 3)) for piece in [latent] + arrived]

    mid_rows = jnp.transpose(mid_filters, (0, 1, 2, 4, 3))
    if divided:
        mine = call(
            functools.partial(pick_kernel, groups),
            jax.ShapeDtypeStruct((3, 3, 3, share, depth1), BF16),
            [pltpu.VMEM(mid_rows.shape, BF16), pltpu.SemaphoreType.DMA],
            6 * 10**9,
            10**6,
            mid_rows,
            stay=(0,),
        )
        mine = [mine] + [exchange(mine, "tile", k) for k in range(2, tiles, 2)]
        mine = jnp.stack(mine)
    else:
        every = lax.all_gather(mid_rows, "tile", axis=3, tiled=True)
        mine = lax.dynamic_slice_in_dim(every, me * share, share, axis=3)[None]

    part = call(
        functools.partial(coarse_kernel, groups),
        jax.ShapeDtypeStruct((cols + 2, cells, width0), BF16),
        [pltpu.VMEM((3, height + 2, cols * frames, depth0), BF16)],
        2 * 27 * cells * cols * depth0 * width0,
        5 * 10**6,
        *pieces,
        coarse_filters,
    )
    straight = call(
        functools.partial(straight_kernel, groups),
        jax.ShapeDtypeStruct((cols, height, frames, depth1), F32),
        [],
        2 * cells * cols * depth0 * depth1,
        10**6,
        *pieces,
        coarse_proj,
    )
    parts = [part] + [exchange(part, "grp", k) for k in range(1, groups)]
    own, even_out, odd_out = call(
        functools.partial(project_kernel, groups),
        (
            jax.ShapeDtypeStruct((cols + 2, cells, depth1), F32),
            jax.ShapeDtypeStruct((2, cells, depth1), BF16),
            jax.ShapeDtypeStruct((2, cells, depth1), BF16),
        ),
        [],
        2 * cells * (cols + 2) * depth0 * depth1,
        2 * 10**6,
        *parts,
        coarse_proj,
        straight,
    )
    if divided:
        later, _ = lax.optimization_barrier((mine, own))
        mine = jnp.concatenate([mine, exchange(later, "tile", 1)])
    mid_folded = call(
        fold_middle_kernel,
        jax.ShapeDtypeStruct((3, 3, 2, depth1, lanes), BF16),
        [],
        10**6,
        4 * 10**6,
        mine,
    )
    odd_pairs = [(i, i + 1) for i in range(1, tiles - 1, 2)]
    even_in = exchange(even_out, "tile", 1)
    odd_in = lax.ppermute(odd_out, "tile", odd_pairs + [(j, i) for i, j in odd_pairs])
    local = (rows + 2) * frames
    *chunks, block = call(
        functools.partial(middle_kernel, groups, rows, frames),
        tuple(jax.ShapeDtypeStruct((cols + 1, local, lanes), BF16) for _ in range(groups))
        + (jax.ShapeDtypeStruct((cols + 2, local, depth1), BF16),),
        [
            pltpu.VMEM((3, cols + 2, cells + 2 * frames, depth1), BF16),
            pltpu.VMEM((3, cols + 2, cells, depth1), BF16),
            pltpu.VMEM((cols + 2, height + 2, frames, depth1), F32),
            pltpu.VMEM((cols + 1, height + 2, frames, lanes), F32),
        ],
        2 * 18 * (cols + 1) * cells * depth1 * lanes,
        5 * 10**6,
        own,
        even_in,
        odd_in,
        mid_folded,
    )
    chunks = [chunks[0]] + [exchange(chunks[k], "grp", k) for k in range(1, groups)]
    fine_folded, spread = call(
        functools.partial(prepare_kernel, groups, shares),
        (
            jax.ShapeDtypeStruct((3, 2, 2, 2 * depth2, 2 * depth2), BF16),
            jax.ShapeDtypeStruct((groups, lanes, 4 * depth2), BF16),
        ),
        [pltpu.VMEM((depth1, depth2), F32)],
        10**6,
        4 * 10**6,
        fine_filters,
        mid_proj,
    )
    tall, broad = 2 * rows, 2 * cols
    return call(
        functools.partial(fine_kernel, groups, frames),
        jax.ShapeDtypeStruct((frames, 2 * tall, 2 * broad, depth2), BF16),
        [
            pltpu.VMEM((3, broad + 2, (tall + 2) * frames, depth2), BF16),
            pltpu.VMEM((3, broad + 2, tall * frames, depth2), BF16),
            pltpu.VMEM((broad + 2, tall, frames, depth2), F32),
        ],
        2 * 24 * (broad + 1) * tall * frames * depth2 * 2 * depth2,
        3 * 10**6,
        *chunks,
        block,
        spread,
        mid_proj,
        fine_folded,
    )


def solution(mesh):
    in_specs = (
        P(None, "grp", "tile", None),
        P(None, None, None, None, "grp"),
        P(None, None, None, None, "tile"),
        P(),
        P(),
        P(),
    )
    out_specs = P(None, "grp", "tile", None)
    return jax.shard_map(body, mesh=mesh, in_specs=in_specs, out_specs=out_specs, check_vma=False)
```

```python
import functools

import jax
import jax.numpy as jnp
from jax import lax
from jax.experimental import pallas as pl
from jax.experimental.pallas import tpu as pltpu
from jax.sharding import PartitionSpec as P

VMEM = pl.BlockSpec(memory_space=pltpu.VMEM)
FAR = pl.BlockSpec(memory_space=pltpu.HBM)
F32 = jnp.float32
BF16 = jnp.bfloat16


def call(kernel, outs, scratch, flops, nbytes, *args, stay=()):
    args = [
        pltpu.with_memory_space_constraint(arg, pltpu.HBM) if n in stay else arg
        for n, arg in enumerate(args)
    ]
    return pl.pallas_call(
        kernel,
        out_shape=outs,
        in_specs=[FAR if n in stay else VMEM for n in range(len(args))],
        out_specs=jax.tree.map(lambda _: VMEM, outs),
        scratch_shapes=scratch,
        compiler_params=pltpu.CompilerParams(vmem_limit_bytes=40 << 20),
        cost_estimate=pl.CostEstimate(flops=flops, bytes_accessed=nbytes, transcendentals=0),
    )(*args)


def dot(left, right):
    return jnp.dot(left, right, preferred_element_type=F32)


def activate(values):
    scaled = values * lax.rsqrt(jnp.mean(values * values, axis=-1, keepdims=True) + 1e-06)
    return scaled / (1.0 + jnp.exp(-scaled))


def delayed(values, steps):
    if steps == 0:
        return values
    axis = values.ndim - 2
    frame = lax.broadcasted_iota(jnp.int32, values.shape, axis)
    return jnp.where(frame >= steps, pltpu.roll(values, steps, axis), 0.0)


def coarse_kernel(groups, *refs):
    pieces, (filters, part, shifted) = refs[:groups], refs[groups:]
    rows, cols, frames, depth = pieces[0].shape
    width = filters.shape[4]
    height = groups * rows
    me = lax.axis_index("grp")
    edge = jnp.zeros((1, cols * frames, depth), BF16)
    for step in range(3):
        shifted[step, 0:1] = edge
        shifted[step, height + 1 : height + 2] = edge
    for k in range(groups):
        at = (me ^ k) * rows
        raw = pieces[k][...]
        act = activate(raw.astype(F32))
        for step in range(3):
            moved = delayed(act, 2 - step).reshape(rows, cols * frames, depth)
            shifted[step, pl.ds(at + 1, rows)] = moved.astype(BF16)
    joined = width % 128 == 0
    totals = [None] * (1 if joined else 3)
    for step in range(3):
        for row in range(3):
            left = shifted[step, row : row + height].reshape(height * cols * frames, depth)
            taps = [filters[step, row, col] for col in range(3)]
            if joined:
                taps = [jnp.concatenate(taps, axis=1)]
            for n, tap in enumerate(taps):
                term = dot(left, tap)
                totals[n] = term if totals[n] is None else totals[n] + term
    if joined:
        totals = [totals[0][:, n * width : (n + 1) * width] for n in range(3)]
    totals = [total.reshape(height, cols, frames, width) for total in totals]
    for out in range(cols + 2):
        value = sum(
            totals[tap][:, out - 2 + tap] for tap in range(3) if 0 <= out - 2 + tap < cols
        )
        part[out] = value.reshape(height * frames, width).astype(BF16)


def straight_kernel(groups, *refs):
    pieces, (proj, straight) = refs[:groups], refs[groups:]
    rows, cols, frames, depth = pieces[0].shape
    me = lax.axis_index("grp")
    for k in range(groups):
        flat = pieces[k][...].reshape(rows * cols * frames, depth)
        direct = dot(flat, proj[...]).reshape(rows, cols, frames, proj.shape[1])
        for col in range(cols):
            straight[col, pl.ds((me ^ k) * rows, rows)] = direct[:, col]


def project_kernel(groups, *refs):
    parts, (proj, straight, own, even_out, odd_out) = refs[:groups], refs[groups:]
    extent, cells, width = parts[0].shape
    outputs = proj.shape[1]
    me = lax.axis_index("grp")
    total = None
    for k in range(groups):
        weights = proj[pl.ds(pl.multiple_of((me ^ k) * width, width), width)]
        term = dot(parts[k][...].reshape(extent * cells, width), weights)
        total = term if total is None else total + term
    total = total.reshape(extent, cells, outputs)
    cols = extent - 2
    middle = total[1 : cols + 1] + straight[...].reshape(cols, cells, outputs)
    own[0] = total[0]
    own[1 : cols + 1] = middle
    own[cols + 1] = total[cols + 1]
    left = jnp.stack([total[0], middle[0]])
    right = jnp.stack([middle[cols - 1], total[cols + 1]])
    odd = lax.axis_index("tile") % 2 == 1
    even_out[...] = jnp.where(odd, left, right).astype(BF16)
    odd_out[...] = jnp.where(odd, right, left).astype(BF16)


def middle_kernel(groups, rows, frames, own, even_in, odd_in, filters, *refs):
    outs, (block, acts, acts_odd, kept, sums) = refs[:groups], refs[groups:]
    extent, cells, depth = own.shape
    cols = extent - 2
    height = cells // frames
    me = lax.axis_index("grp")
    tile = lax.axis_index("tile")
    odd = tile % 2 == 1
    even_got = even_in[...].astype(F32)
    odd_got = odd_in[...].astype(F32)
    from_left = jnp.where(odd, even_got, odd_got)
    from_right = jnp.where(odd, odd_got, even_got)
    values = []
    for col in range(extent):
        value = own[col]
        if col < 2:
            value = value + from_left[col]
        if col >= cols:
            value = value + from_right[col - cols]
        if col == 0:
            value = jnp.where(tile == 0, 0.0, value)
        if col == extent - 1:
            value = jnp.where(tile == lax.axis_size("tile") - 1, 0.0, value)
        values.append(value.astype(BF16).astype(F32).reshape(height, frames, depth))
    nothing = jnp.zeros((1, frames, depth), F32)
    for col in range(extent):
        kept[col, 0:1] = nothing
        kept[col, 1 : height + 1] = values[col]
        kept[col, height + 1 : height + 2] = nothing
        act = activate(values[col])
        for step in range(3):
            moved = delayed(act, 2 - step)
            framed = jnp.concatenate([nothing, moved, nothing], axis=0)
            acts[step, col] = framed.reshape(cells + 2 * frames, depth).astype(BF16)
            acts_odd[step, col] = moved.reshape(cells, depth).astype(BF16)
    block[...] = (
        kept[:, pl.ds(me * rows, rows + 2)]
        .reshape(extent, (rows + 2) * frames, depth)
        .astype(BF16)
    )
    pairs = extent - 1
    total = None
    for step in range(3):
        for row in range(3):
            for side in range(2):
                if row == 1:
                    left = acts_odd[step, side : side + pairs]
                else:
                    first = row * frames
                    left = acts[step, side : side + pairs, first : first + cells]
                term = dot(left.reshape(pairs * cells, depth), filters[step, row, side])
                total = term if total is None else total + term
    lanes = total.shape[1]
    total = total.reshape(pairs, height, frames, lanes)
    empty = jnp.zeros((pairs, 1, frames, lanes), F32)
    sums[:, 0:1] = empty
    sums[:, 1 : height + 1] = total
    sums[:, height + 1 : height + 2] = empty
    half = lanes // 2
    for k in range(groups):
        chunk = sums[:, pl.ds((me ^ k) * rows, rows + 2)]
        ends = jnp.concatenate([chunk[:, rows + 1 :, :, :half], chunk[:, :1, :, half:]], axis=3)
        chunk = jnp.concatenate([ends, chunk[:, 1 : rows + 1]], axis=1)
        outs[k][...] = chunk.reshape(pairs * (rows + 1) * frames, lanes).astype(BF16)


def fine_kernel(groups, frames, *refs):
    chunks = refs[:groups]
    block, spread, proj, filters, out, acts, acts_odd, lows = refs[groups:]
    extent, cells = block.shape[:2]
    pairs, rows = extent - 1, cells // frames - 2
    width = proj.shape[1]
    tall, broad = 2 * rows, 2 * (extent - 2)
    me, last_me = lax.axis_index("grp"), lax.axis_size("grp") - 1
    tile, last_tile = lax.axis_index("tile"), lax.axis_size("tile") - 1
    total = None
    for k in range(groups):
        term = dot(chunks[k][...], spread[k])
        total = term if total is None else total + term
    total = total.reshape(pairs, rows + 1, frames, 4 * width)
    base = dot(block[...].reshape(extent * cells, block.shape[2]), proj[...])
    base = base.reshape(extent, rows + 2, frames, width)
    nothing = jnp.zeros((1, frames, width), F32)
    for col in range(broad + 2):
        pair, side = divmod(col, 2)
        upper, lower = [
            total[pair, :, :, (2 * p + side) * width : (2 * p + side + 1) * width]
            for p in range(2)
        ]
        lower = lower + base[pair + side, : rows + 1]
        upper = jnp.concatenate([upper[1:], upper[:1]], axis=0) + base[pair + side, 1:]
        woven = jnp.stack([lower, upper], axis=1)
        value = woven.reshape(tall + 2, frames, width).astype(BF16).astype(F32)
        if col == 0:
            value = jnp.where(tile == 0, 0.0, value)
        if col == broad + 1:
            value = jnp.where(tile == last_tile, 0.0, value)
        top = jnp.where(me == 0, 0.0, value[0:1])
        bottom = jnp.where(me == last_me, 0.0, value[tall + 1 : tall + 2])
        value = jnp.concatenate([top, value[1 : tall + 1], bottom], axis=0)
        lows[col] = value[1 : tall + 1]
        act = activate(value)
        for step in range(3):
            moved = delayed(act, 2 - step)
            acts[step, col] = moved.reshape((tall + 2) * frames, width).astype(BF16)
            acts_odd[step, col] = (
                moved[1 : tall + 1].reshape(tall * frames, width).astype(BF16)
            )
    span = broad + 1
    strip = tall * frames
    for p in range(2):
        sums = None
        for step in range(3):
            for near in range(2):
                row = p + near
                if row == 1:
                    pick = [acts_odd[step, side : side + span] for side in range(2)]
                else:
                    first = row * frames
                    pick = [
                        acts[step, side : side + span, first : first + strip]
                        for side in range(2)
                    ]
                left = jnp.concatenate([v.reshape(span * strip, width) for v in pick], axis=1)
                term = dot(left, filters[step, p, near])
                sums = term if sums is None else sums + term
        sums = sums.reshape(span, tall, frames, 2 * width)
        fields = []
        for col in range(2 * broad):
            pair, side = divmod(col + 1, 2)
            low = lows[pair + side]
            fields.append(sums[pair, :, :, side * width : (side + 1) * width] + low)
        field = jnp.stack(fields, axis=1)
        for row in range(tall):
            out[:, 2 * row + p] = jnp.swapaxes(field[row], 0, 1).astype(BF16)


def fold_middle_kernel(pieces, out):
    parts, n, depth = pieces.shape[0], pieces.shape[4], pieces.shape[5]

    def per_step(step, carry):
        taps = [
            [
                pieces[:, step, row, col].astype(F32).reshape(parts * n, depth)
                for col in range(3)
            ]
            for row in range(3)
        ]
        nothing = jnp.zeros((parts * n, depth), F32)
        for side in range(2):
            narrow = [
                [taps[r][0] + taps[r][1] if side == 0 else taps[r][2],
                 taps[r][0] if side == 0 else taps[r][1] + taps[r][2]]
                for r in range(3)
            ]
            for row in range(3):
                blocks = []
                for p in range(2):
                    for q in range(2):
                        if row == 1:
                            value = narrow[1][q] + narrow[2 if p == 0 else 0][q]
                        elif row == 0:
                            value = narrow[0][q] if p == 0 else nothing
                        else:
                            value = nothing if p == 0 else narrow[2][q]
                        blocks.append(value)
                out[step, row, side] = jnp.concatenate(blocks, axis=0).T.astype(BF16)
        return carry

    lax.fori_loop(0, 3, per_step, 0)


def pick_kernel(groups, stored, out, filters, arrived):
    copy = pltpu.make_async_copy(stored, filters, arrived)
    copy.start()
    me = lax.axis_index("grp")
    share = out.shape[3]
    copy.wait()
    value = filters[:, :, :, 0:share].astype(F32)
    for k in range(1, groups):
        value = jnp.where(me == k, filters[:, :, :, k * share : (k + 1) * share].astype(F32), value)
    out[...] = value.astype(BF16)


def prepare_kernel(groups, parts, filters, proj, folded, spread, plain):
    def per_step(step, carry):
        taps = [[filters[step, r, c].astype(F32) for c in range(3)] for r in range(3)]
        for p in range(2):
            for near in range(2):
                if p == 0:
                    line = taps[0] if near == 0 else [x + y for x, y in zip(taps[1], taps[2])]
                else:
                    line = [x + y for x, y in zip(taps[0], taps[1])] if near == 0 else taps[2]
                first = jnp.concatenate([line[0] + line[1], line[0]], axis=1)
                second = jnp.concatenate([line[2], line[1] + line[2]], axis=1)
                folded[step, p, near] = jnp.concatenate([first, second], axis=0).astype(BF16)
        return carry

    lax.fori_loop(0, 3, per_step, 0)
    depth, width = proj.shape
    plain[...] = proj[...].astype(F32)
    me, tile = lax.axis_index("grp"), lax.axis_index("tile")
    share = depth // (groups * parts)
    spread[...] = jnp.zeros(spread.shape, BF16)
    for k in range(groups):
        lines = []
        for s in range(parts):
            if parts == 1:
                first = (me ^ k) * share
            else:
                source = tile ^ (s // (parts // 2)) ^ (2 * (s % (parts // 2)))
                first = (source * groups + (me ^ k)) * share
            lines.append(plain[pl.ds(pl.multiple_of(first, 8), share)])
        block = jnp.concatenate(lines, axis=0).astype(BF16)
        height = parts * share
        for phase in range(4):
            spread[
                k, phase * height : (phase + 1) * height, phase * width : (phase + 1) * width
            ] = block


def exchange(values, axis, k):
    size = lax.axis_size(axis)
    return lax.ppermute(values, axis, [(i, i ^ k) for i in range(size)])


def body(latent, coarse_filters, mid_filters, fine_filters, coarse_proj, mid_proj):
    groups, tiles = lax.axis_size("grp"), lax.axis_size("tile")
    me, tile = lax.axis_index("grp"), lax.axis_index("tile")
    frames, rows, cols, depth0 = latent.shape
    depth1, depth2 = mid_proj.shape
    width0 = coarse_filters.shape[4]
    height = groups * rows
    cells = height * frames
    own_mid = mid_filters.shape[4]

    divided = own_mid % groups == 0 and (own_mid // groups) % 8 == 0
    share, shares = (own_mid // groups, tiles) if divided else (depth1 // groups, 1)
    lanes = 4 * shares * share
    arrived = [exchange(latent, "grp", k) for k in range(1, groups)]
    arrived = lax.optimization_barrier(arrived)
    pieces = [jnp.transpose(piece, (1, 2, 0, 3)) for piece in [latent] + arrived]

    mid_rows = jnp.transpose(mid_filters, (0, 1, 2, 4, 3))
    if divided:
        mine = call(
            functools.partial(pick_kernel, groups),
            jax.ShapeDtypeStruct((3, 3, 3, share, depth1), BF16),
            [pltpu.VMEM(mid_rows.shape, BF16), pltpu.SemaphoreType.DMA],
            6 * 10**9,
            10**6,
            mid_rows,
            stay=(0,),
        )
        mine, bit = mine[None], 2
        while 2 * bit < tiles:
            mine = jnp.concatenate([mine, exchange(mine, "tile", bit)])
            bit *= 2
        beyond = exchange(mine, "tile", bit)
    else:
        every = lax.all_gather(mid_rows, "tile", axis=3, tiled=True)
        mine = lax.dynamic_slice_in_dim(every, me * share, share, axis=3)[None]

    part = call(
        functools.partial(coarse_kernel, groups),
        jax.ShapeDtypeStruct((cols + 2, cells, width0), BF16),
        [pltpu.VMEM((3, height + 2, cols * frames, depth0), BF16)],
        5 * 10**8,
        10**5,
        *pieces,
        coarse_filters,
    )
    straight = call(
        functools.partial(straight_kernel, groups),
        jax.ShapeDtypeStruct((cols, height, frames, depth1), F32),
        [],
        2 * cells * cols * depth0 * depth1,
        10**6,
        *pieces,
        coarse_proj,
    )
    parts = [part] + [exchange(part, "grp", k) for k in range(1, groups)]
    own, even_out, odd_out = call(
        functools.partial(project_kernel, groups),
        (
            jax.ShapeDtypeStruct((cols + 2, cells, depth1), F32),
            jax.ShapeDtypeStruct((2, cells, depth1), BF16),
            jax.ShapeDtypeStruct((2, cells, depth1), BF16),
        ),
        [],
        2 * cells * (cols + 2) * depth0 * depth1,
        2 * 10**6,
        *parts,
        coarse_proj,
        straight,
    )
    if divided:
        beyond, _ = lax.optimization_barrier((beyond, own))
        mine = jnp.concatenate([mine, beyond])
        mine = jnp.concatenate([mine, exchange(mine, "tile", 1)])
    mid_folded = call(
        fold_middle_kernel,
        jax.ShapeDtypeStruct((3, 3, 2, depth1, lanes), BF16),
        [],
        10**6,
        4 * 10**6,
        mine,
    )
    odd_pairs = [(i, i + 1) for i in range(1, tiles - 1, 2)]
    even_in = exchange(even_out, "tile", 1)
    odd_in = lax.ppermute(odd_out, "tile", odd_pairs + [(j, i) for i, j in odd_pairs])
    local = (rows + 2) * frames
    *chunks, block = call(
        functools.partial(middle_kernel, groups, rows, frames),
        tuple(
            jax.ShapeDtypeStruct(((cols + 1) * (rows + 1) * frames, lanes), BF16)
            for _ in range(groups)
        )
        + (jax.ShapeDtypeStruct((cols + 2, local, depth1), BF16),),
        [
            pltpu.VMEM((3, cols + 2, cells + 2 * frames, depth1), BF16),
            pltpu.VMEM((3, cols + 2, cells, depth1), BF16),
            pltpu.VMEM((cols + 2, height + 2, frames, depth1), F32),
            pltpu.VMEM((cols + 1, height + 2, frames, lanes), F32),
        ],
        2 * 18 * (cols + 1) * cells * depth1 * lanes,
        5 * 10**6,
        own,
        even_in,
        odd_in,
        mid_folded,
    )
    chunks = [chunks[0]] + [exchange(chunks[k], "grp", k) for k in range(1, groups)]
    fine_folded, spread = call(
        functools.partial(prepare_kernel, groups, shares),
        (
            jax.ShapeDtypeStruct((3, 2, 2, 2 * depth2, 2 * depth2), BF16),
            jax.ShapeDtypeStruct((groups, lanes, 4 * depth2), BF16),
        ),
        [pltpu.VMEM((depth1, depth2), F32)],
        10**6,
        4 * 10**6,
        fine_filters,
        mid_proj,
    )
    tall, broad = 2 * rows, 2 * cols
    return call(
        functools.partial(fine_kernel, groups, frames),
        jax.ShapeDtypeStruct((frames, 2 * tall, 2 * broad, depth2), BF16),
        [
            pltpu.VMEM((3, broad + 2, (tall + 2) * frames, depth2), BF16),
            pltpu.VMEM((3, broad + 2, tall * frames, depth2), BF16),
            pltpu.VMEM((broad + 2, tall, frames, depth2), F32),
        ],
        2 * 24 * (broad + 1) * tall * frames * depth2 * 2 * depth2,
        3 * 10**6,
        *chunks,
        block,
        spread,
        mid_proj,
        fine_folded,
    )


def solution(mesh):
    in_specs = (
        P(None, "grp", "tile", None),
        P(None, None, None, None, "grp"),
        P(None, None, None, None, "tile"),
        P(),
        P(),
        P(),
    )
    out_specs = P(None, "grp", "tile", None)
    return jax.shard_map(body, mesh=mesh, in_specs=in_specs, out_specs=out_specs, check_vma=False)
```

```python
import functools

import jax
import jax.numpy as jnp
from jax import lax
from jax.experimental import pallas as pl
from jax.experimental.layout import Layout, with_layout_constraint
from jax.experimental.pallas import tpu as pltpu
from jax.sharding import PartitionSpec as P

VMEM = pl.BlockSpec(memory_space=pltpu.VMEM)
FAR = pl.BlockSpec(memory_space=pltpu.HBM)
F32 = jnp.float32
BF16 = jnp.bfloat16


def call(kernel, outs, scratch, flops, nbytes, *args, stay=()):
    args = [
        pltpu.with_memory_space_constraint(arg, pltpu.HBM) if n in stay else arg
        for n, arg in enumerate(args)
    ]
    return pl.pallas_call(
        kernel,
        out_shape=outs,
        in_specs=[FAR if n in stay else VMEM for n in range(len(args))],
        out_specs=jax.tree.map(lambda _: VMEM, outs),
        scratch_shapes=scratch,
        compiler_params=pltpu.CompilerParams(vmem_limit_bytes=40 << 20),
        cost_estimate=pl.CostEstimate(flops=flops, bytes_accessed=nbytes, transcendentals=0),
    )(*args)


def dot(left, right):
    return jnp.dot(left, right, preferred_element_type=F32)


def activate(values):
    scaled = values * lax.rsqrt(jnp.mean(values * values, axis=-1, keepdims=True) + 1e-06)
    return scaled / (1.0 + jnp.exp(-scaled))


def delayed(values, steps):
    if steps == 0:
        return values
    axis = values.ndim - 2
    frame = lax.broadcasted_iota(jnp.int32, values.shape, axis)
    return jnp.where(frame >= steps, pltpu.roll(values, steps, axis), 0.0)


def coarse_kernel(groups, *refs):
    pieces, (filters, part, shifted) = refs[:groups], refs[groups:]
    rows, cols, frames, depth = pieces[0].shape
    width = filters.shape[4]
    height = groups * rows
    me = lax.axis_index("grp")
    edge = jnp.zeros((1, cols * frames, depth), BF16)
    for step in range(3):
        shifted[step, 0:1] = edge
        shifted[step, height + 1 : height + 2] = edge
    for k in range(groups):
        at = (me ^ k) * rows
        raw = pieces[k][...]
        act = activate(raw.astype(F32))
        for step in range(3):
            moved = delayed(act, 2 - step).reshape(rows, cols * frames, depth)
            shifted[step, pl.ds(at + 1, rows)] = moved.astype(BF16)
    joined = width % 128 == 0
    totals = [None] * (1 if joined else 3)
    for step in range(3):
        for row in range(3):
            left = shifted[step, row : row + height].reshape(height * cols * frames, depth)
            taps = [filters[step, row, col] for col in range(3)]
            if joined:
                taps = [jnp.concatenate(taps, axis=1)]
            for n, tap in enumerate(taps):
                term = dot(left, tap)
                totals[n] = term if totals[n] is None else totals[n] + term
    if joined:
        totals = [totals[0][:, n * width : (n + 1) * width] for n in range(3)]
    totals = [total.reshape(height, cols, frames, width) for total in totals]
    for out in range(cols + 2):
        value = sum(
            totals[tap][:, out - 2 + tap] for tap in range(3) if 0 <= out - 2 + tap < cols
        )
        part[out] = value.reshape(height * frames, width).astype(BF16)


def straight_kernel(groups, *refs):
    pieces, (proj, straight) = refs[:groups], refs[groups:]
    rows, cols, frames, depth = pieces[0].shape
    me = lax.axis_index("grp")
    for k in range(groups):
        flat = pieces[k][...].reshape(rows * cols * frames, depth)
        direct = dot(flat, proj[...]).reshape(rows, cols, frames, proj.shape[1])
        for col in range(cols):
            straight[col, pl.ds((me ^ k) * rows, rows)] = direct[:, col]


def project_kernel(groups, *refs):
    parts, (proj, straight, odd_out, even_out, own) = refs[:groups], refs[groups:]
    extent, cells, width = parts[0].shape
    outputs = proj.shape[1]
    me = lax.axis_index("grp")
    total = None
    for k in range(groups):
        weights = proj[pl.ds(pl.multiple_of((me ^ k) * width, width), width)]
        term = dot(parts[k][...].reshape(extent * cells, width), weights)
        total = term if total is None else total + term
    total = total.reshape(extent, cells, outputs)
    cols = extent - 2
    middle = total[1 : cols + 1] + straight[...].reshape(cols, cells, outputs)
    own[0] = total[0]
    own[1 : cols + 1] = middle
    own[cols + 1] = total[cols + 1]
    left = jnp.stack([total[0], middle[0]])
    right = jnp.stack([middle[cols - 1], total[cols + 1]])
    odd = lax.axis_index("tile") % 2 == 1
    even_out[...] = jnp.where(odd, left, right).astype(BF16)
    odd_out[...] = jnp.where(odd, right, left).astype(BF16)


def middle_kernel(groups, rows, frames, odd_in, even_in, own, filters, *refs):
    outs, (block, acts, acts_odd, kept, sums) = refs[:groups], refs[groups:]
    extent, cells, depth = own.shape
    cols = extent - 2
    height = cells // frames
    me = lax.axis_index("grp")
    tile = lax.axis_index("tile")
    odd = tile % 2 == 1
    even_got = even_in[...].astype(F32)
    odd_got = odd_in[...].astype(F32)
    from_left = jnp.where(odd, even_got, odd_got)
    from_right = jnp.where(odd, odd_got, even_got)
    values = []
    for col in range(extent):
        value = own[col]
        if col < 2:
            value = value + from_left[col]
        if col >= cols:
            value = value + from_right[col - cols]
        if col == 0:
            value = jnp.where(tile == 0, 0.0, value)
        if col == extent - 1:
            value = jnp.where(tile == lax.axis_size("tile") - 1, 0.0, value)
        values.append(value.astype(BF16).astype(F32).reshape(height, frames, depth))
    nothing = jnp.zeros((1, frames, depth), F32)
    for col in range(extent):
        kept[col, 0:1] = nothing
        kept[col, 1 : height + 1] = values[col]
        kept[col, height + 1 : height + 2] = nothing
        act = activate(values[col])
        for step in range(3):
            moved = delayed(act, 2 - step)
            framed = jnp.concatenate([nothing, moved, nothing], axis=0)
            acts[step, col] = framed.reshape(cells + 2 * frames, depth).astype(BF16)
            acts_odd[step, col] = moved.reshape(cells, depth).astype(BF16)
    block[...] = (
        kept[:, pl.ds(me * rows, rows + 2)]
        .reshape(extent, (rows + 2) * frames, depth)
        .astype(BF16)
    )
    pairs = extent - 1
    total = None
    for step in range(3):
        for row in range(3):
            for side in range(2):
                if row == 1:
                    left = acts_odd[step, side : side + pairs]
                else:
                    first = row * frames
                    left = acts[step, side : side + pairs, first : first + cells]
                term = dot(left.reshape(pairs * cells, depth), filters[step, row, side])
                total = term if total is None else total + term
    lanes = total.shape[1]
    total = total.reshape(pairs, height, frames, lanes)
    empty = jnp.zeros((pairs, 1, frames, lanes), F32)
    sums[:, 0:1] = empty
    sums[:, 1 : height + 1] = total
    sums[:, height + 1 : height + 2] = empty
    half = lanes // 2
    for k in range(groups):
        chunk = sums[:, pl.ds((me ^ k) * rows, rows + 2)]
        ends = jnp.concatenate([chunk[:, rows + 1 :, :, :half], chunk[:, :1, :, half:]], axis=3)
        chunk = jnp.concatenate([ends, chunk[:, 1 : rows + 1]], axis=1)
        outs[k][...] = chunk.reshape(pairs * (rows + 1) * frames, lanes).astype(BF16)


def fine_kernel(groups, frames, *refs):
    chunks = refs[:groups]
    block, spread, proj, filters, out, acts, acts_odd, lows = refs[groups:]
    extent, cells = block.shape[:2]
    pairs, rows = extent - 1, cells // frames - 2
    width = proj.shape[1]
    tall, broad = 2 * rows, 2 * (extent - 2)
    me, last_me = lax.axis_index("grp"), lax.axis_size("grp") - 1
    tile, last_tile = lax.axis_index("tile"), lax.axis_size("tile") - 1
    total = None
    for k in range(groups):
        term = dot(chunks[k][...], spread[k])
        total = term if total is None else total + term
    total = total.reshape(pairs, rows + 1, frames, 4 * width)
    base = dot(block[...].reshape(extent * cells, block.shape[2]), proj[...])
    base = base.reshape(extent, rows + 2, frames, width)
    nothing = jnp.zeros((1, frames, width), F32)
    for col in range(broad + 2):
        pair, side = divmod(col, 2)
        upper, lower = [
            total[pair, :, :, (2 * p + side) * width : (2 * p + side + 1) * width]
            for p in range(2)
        ]
        lower = lower + base[pair + side, : rows + 1]
        upper = jnp.concatenate([upper[1:], upper[:1]], axis=0) + base[pair + side, 1:]
        woven = jnp.stack([lower, upper], axis=1)
        value = woven.reshape(tall + 2, frames, width).astype(BF16).astype(F32)
        if col == 0:
            value = jnp.where(tile == 0, 0.0, value)
        if col == broad + 1:
            value = jnp.where(tile == last_tile, 0.0, value)
        top = jnp.where(me == 0, 0.0, value[0:1])
        bottom = jnp.where(me == last_me, 0.0, value[tall + 1 : tall + 2])
        value = jnp.concatenate([top, value[1 : tall + 1], bottom], axis=0)
        lows[col] = value[1 : tall + 1]
        act = activate(value)
        for step in range(3):
            moved = delayed(act, 2 - step)
            acts[step, col] = moved.reshape((tall + 2) * frames, width).astype(BF16)
            acts_odd[step, col] = (
                moved[1 : tall + 1].reshape(tall * frames, width).astype(BF16)
            )
    span = broad + 1
    strip = tall * frames
    for p in range(2):
        sums = None
        for step in range(3):
            for near in range(2):
                row = p + near
                if row == 1:
                    pick = [acts_odd[step, side : side + span] for side in range(2)]
                else:
                    first = row * frames
                    pick = [
                        acts[step, side : side + span, first : first + strip]
                        for side in range(2)
                    ]
                left = jnp.concatenate([v.reshape(span * strip, width) for v in pick], axis=1)
                term = dot(left, filters[step, p, near])
                sums = term if sums is None else sums + term
        sums = sums.reshape(span, tall, frames, 2 * width)
        fields = []
        for col in range(2 * broad):
            pair, side = divmod(col + 1, 2)
            low = lows[pair + side]
            fields.append(sums[pair, :, :, side * width : (side + 1) * width] + low)
        field = jnp.stack(fields, axis=1)
        for row in range(tall):
            out[:, 2 * row + p] = jnp.swapaxes(field[row], 0, 1).astype(BF16)


def fold_middle_kernel(pieces, out):
    parts, n, depth = pieces.shape[0], pieces.shape[4], pieces.shape[5]

    def per_step(step, carry):
        taps = [
            [
                pieces[:, step, row, col].astype(F32).reshape(parts * n, depth)
                for col in range(3)
            ]
            for row in range(3)
        ]
        nothing = jnp.zeros((parts * n, depth), F32)
        for side in range(2):
            narrow = [
                [taps[r][0] + taps[r][1] if side == 0 else taps[r][2],
                 taps[r][0] if side == 0 else taps[r][1] + taps[r][2]]
                for r in range(3)
            ]
            for row in range(3):
                blocks = []
                for p in range(2):
                    for q in range(2):
                        if row == 1:
                            value = narrow[1][q] + narrow[2 if p == 0 else 0][q]
                        elif row == 0:
                            value = narrow[0][q] if p == 0 else nothing
                        else:
                            value = nothing if p == 0 else narrow[2][q]
                        blocks.append(value)
                out[step, row, side] = jnp.concatenate(blocks, axis=0).T.astype(BF16)
        return carry

    lax.fori_loop(0, 3, per_step, 0)


def pick_kernel(groups, stored, out, filters, arrived):
    copy = pltpu.make_async_copy(stored, filters, arrived)
    copy.start()
    me = lax.axis_index("grp")
    share = out.shape[3]
    copy.wait()
    value = filters[:, :, :, 0:share].astype(F32)
    for k in range(1, groups):
        value = jnp.where(me == k, filters[:, :, :, k * share : (k + 1) * share].astype(F32), value)
    out[...] = value.astype(BF16)


def prepare_kernel(groups, parts, filters, proj, folded, spread, plain):
    def per_step(step, carry):
        taps = [[filters[step, r, c].astype(F32) for c in range(3)] for r in range(3)]
        for p in range(2):
            for near in range(2):
                if p == 0:
                    line = taps[0] if near == 0 else [x + y for x, y in zip(taps[1], taps[2])]
                else:
                    line = [x + y for x, y in zip(taps[0], taps[1])] if near == 0 else taps[2]
                first = jnp.concatenate([line[0] + line[1], line[0]], axis=1)
                second = jnp.concatenate([line[2], line[1] + line[2]], axis=1)
                folded[step, p, near] = jnp.concatenate([first, second], axis=0).astype(BF16)
        return carry

    lax.fori_loop(0, 3, per_step, 0)
    depth, width = proj.shape
    plain[...] = proj[...].astype(F32)
    me, tile = lax.axis_index("grp"), lax.axis_index("tile")
    share = depth // (groups * parts)
    spread[...] = jnp.zeros(spread.shape, BF16)
    for k in range(groups):
        lines = []
        for s in range(parts):
            if parts == 1:
                first = (me ^ k) * share
            else:
                source = tile ^ (s // (parts // 2)) ^ (2 * (s % (parts // 2)))
                first = (source * groups + (me ^ k)) * share
            lines.append(plain[pl.ds(pl.multiple_of(first, 8), share)])
        block = jnp.concatenate(lines, axis=0).astype(BF16)
        height = parts * share
        for phase in range(4):
            spread[
                k, phase * height : (phase + 1) * height, phase * width : (phase + 1) * width
            ] = block


def exchange(values, axis, k):
    size = lax.axis_size(axis)
    return lax.ppermute(values, axis, [(i, i ^ k) for i in range(size)])


def body(latent, coarse_filters, mid_filters, fine_filters, coarse_proj, mid_proj):
    groups, tiles = lax.axis_size("grp"), lax.axis_size("tile")
    me, tile = lax.axis_index("grp"), lax.axis_index("tile")
    frames, rows, cols, depth0 = latent.shape
    depth1, depth2 = mid_proj.shape
    width0 = coarse_filters.shape[4]
    height = groups * rows
    cells = height * frames
    own_mid = mid_filters.shape[4]

    divided = own_mid % groups == 0 and (own_mid // groups) % 8 == 0
    share, shares = (own_mid // groups, tiles) if divided else (depth1 // groups, 1)
    lanes = 4 * shares * share
    arrived = [exchange(latent, "grp", k) for k in range(1, groups)]
    arrived = [with_layout_constraint(piece, Layout((0, 1, 2, 3))) for piece in arrived]
    pieces = [jnp.transpose(piece, (1, 2, 0, 3)) for piece in [latent] + arrived]

    mid_rows = jnp.transpose(mid_filters, (0, 1, 2, 4, 3))
    if divided:
        mine = call(
            functools.partial(pick_kernel, groups),
            jax.ShapeDtypeStruct((3, 3, 3, share, depth1), BF16),
            [pltpu.VMEM(mid_rows.shape, BF16), pltpu.SemaphoreType.DMA],
            6 * 10**9,
            10**6,
            mid_rows,
            stay=(0,),
        )
        mine, bit = mine[None], 2
        while 2 * bit < tiles:
            mine = jnp.concatenate([mine, exchange(mine, "tile", bit)])
            bit *= 2
        beyond = exchange(mine, "tile", bit)
    else:
        every = lax.all_gather(mid_rows, "tile", axis=3, tiled=True)
        mine = lax.dynamic_slice_in_dim(every, me * share, share, axis=3)[None]

    part = call(
        functools.partial(coarse_kernel, groups),
        jax.ShapeDtypeStruct((cols + 2, cells, width0), BF16),
        [pltpu.VMEM((3, height + 2, cols * frames, depth0), BF16)],
        5 * 10**8,
        10**5,
        *pieces,
        coarse_filters,
    )
    straight = call(
        functools.partial(straight_kernel, groups),
        jax.ShapeDtypeStruct((cols, height, frames, depth1), F32),
        [],
        2 * cells * cols * depth0 * depth1,
        10**6,
        *pieces,
        coarse_proj,
    )
    parts = [part] + [exchange(part, "grp", k) for k in range(1, groups)]
    odd_out, even_out, own = call(
        functools.partial(project_kernel, groups),
        (
            jax.ShapeDtypeStruct((2, cells, depth1), BF16),
            jax.ShapeDtypeStruct((2, cells, depth1), BF16),
            jax.ShapeDtypeStruct((cols + 2, cells, depth1), F32),
        ),
        [],
        2 * cells * (cols + 2) * depth0 * depth1,
        2 * 10**6,
        *parts,
        coarse_proj,
        straight,
    )
    odd_pairs = [(i, i + 1) for i in range(1, tiles - 1, 2)]
    odd_in = lax.ppermute(odd_out, "tile", odd_pairs + [(j, i) for i, j in odd_pairs])
    even_in = exchange(even_out, "tile", 1)
    if divided:
        beyond, _ = lax.optimization_barrier((beyond, own))
        mine = jnp.concatenate([mine, beyond])
        mine = jnp.concatenate([mine, exchange(mine, "tile", 1)])
    mid_folded = call(
        fold_middle_kernel,
        jax.ShapeDtypeStruct((3, 3, 2, depth1, lanes), BF16),
        [],
        10**6,
        4 * 10**6,
        mine,
    )
    local = (rows + 2) * frames
    *chunks, block = call(
        functools.partial(middle_kernel, groups, rows, frames),
        tuple(
            jax.ShapeDtypeStruct(((cols + 1) * (rows + 1) * frames, lanes), BF16)
            for _ in range(groups)
        )
        + (jax.ShapeDtypeStruct((cols + 2, local, depth1), BF16),),
        [
            pltpu.VMEM((3, cols + 2, cells + 2 * frames, depth1), BF16),
            pltpu.VMEM((3, cols + 2, cells, depth1), BF16),
            pltpu.VMEM((cols + 2, height + 2, frames, depth1), F32),
            pltpu.VMEM((cols + 1, height + 2, frames, lanes), F32),
        ],
        2 * 18 * (cols + 1) * cells * depth1 * lanes,
        5 * 10**6,
        odd_in,
        even_in,
        own,
        mid_folded,
    )
    chunks = [chunks[0]] + [exchange(chunks[k], "grp", k) for k in range(1, groups)]
    fine_folded, spread = call(
        functools.partial(prepare_kernel, groups, shares),
        (
            jax.ShapeDtypeStruct((3, 2, 2, 2 * depth2, 2 * depth2), BF16),
            jax.ShapeDtypeStruct((groups, lanes, 4 * depth2), BF16),
        ),
        [pltpu.VMEM((depth1, depth2), F32)],
        10**6,
        4 * 10**6,
        fine_filters,
        mid_proj,
    )
    tall, broad = 2 * rows, 2 * cols
    return call(
        functools.partial(fine_kernel, groups, frames),
        jax.ShapeDtypeStruct((frames, 2 * tall, 2 * broad, depth2), BF16),
        [
            pltpu.VMEM((3, broad + 2, (tall + 2) * frames, depth2), BF16),
            pltpu.VMEM((3, broad + 2, tall * frames, depth2), BF16),
            pltpu.VMEM((broad + 2, tall, frames, depth2), F32),
        ],
        2 * 24 * (broad + 1) * tall * frames * depth2 * 2 * depth2,
        3 * 10**6,
        *chunks,
        block,
        spread,
        mid_proj,
        fine_folded,
    )


def solution(mesh):
    in_specs = (
        P(None, "grp", "tile", None),
        P(None, None, None, None, "grp"),
        P(None, None, None, None, "tile"),
        P(),
        P(),
        P(),
    )
    out_specs = P(None, "grp", "tile", None)
    return jax.shard_map(body, mesh=mesh, in_specs=in_specs, out_specs=out_specs, check_vma=False)
```

```python
import functools

import jax
import jax.numpy as jnp
from jax import lax
from jax.experimental import pallas as pl
from jax.experimental.layout import Layout, with_layout_constraint
from jax.experimental.pallas import tpu as pltpu
from jax.sharding import PartitionSpec as P

VMEM = pl.BlockSpec(memory_space=pltpu.VMEM)
FAR = pl.BlockSpec(memory_space=pltpu.HBM)
F32 = jnp.float32
BF16 = jnp.bfloat16


def call(kernel, outs, scratch, flops, nbytes, *args, stay=()):
    args = [
        pltpu.with_memory_space_constraint(arg, pltpu.HBM) if n in stay else arg
        for n, arg in enumerate(args)
    ]
    return pl.pallas_call(
        kernel,
        out_shape=outs,
        in_specs=[FAR if n in stay else VMEM for n in range(len(args))],
        out_specs=jax.tree.map(lambda _: VMEM, outs),
        scratch_shapes=scratch,
        compiler_params=pltpu.CompilerParams(vmem_limit_bytes=40 << 20),
        cost_estimate=pl.CostEstimate(flops=flops, bytes_accessed=nbytes, transcendentals=0),
    )(*args)


def dot(left, right):
    return jnp.dot(left, right, preferred_element_type=F32)


def activate(values):
    scaled = values * lax.rsqrt(jnp.mean(values * values, axis=-1, keepdims=True) + 1e-06)
    return scaled / (1.0 + jnp.exp(-scaled))


def delayed(values, steps):
    if steps == 0:
        return values
    axis = values.ndim - 2
    frame = lax.broadcasted_iota(jnp.int32, values.shape, axis)
    return jnp.where(frame >= steps, pltpu.roll(values, steps, axis), 0.0)


def coarse_kernel(groups, *refs):
    pieces, (filters, part, shifted) = refs[:groups], refs[groups:]
    rows, cols, frames, depth = pieces[0].shape
    width = filters.shape[4]
    height = groups * rows
    me = lax.axis_index("grp")
    edge = jnp.zeros((1, cols * frames, depth), BF16)
    for step in range(3):
        shifted[step, 0:1] = edge
        shifted[step, height + 1 : height + 2] = edge
    for k in range(groups):
        at = (me ^ k) * rows
        raw = pieces[k][...]
        act = activate(raw.astype(F32))
        for step in range(3):
            moved = delayed(act, 2 - step).reshape(rows, cols * frames, depth)
            shifted[step, pl.ds(at + 1, rows)] = moved.astype(BF16)
    joined = width % 128 == 0
    totals = [None] * (1 if joined else 3)
    for step in range(3):
        for row in range(3):
            left = shifted[step, row : row + height].reshape(height * cols * frames, depth)
            taps = [filters[step, row, col] for col in range(3)]
            if joined:
                taps = [jnp.concatenate(taps, axis=1)]
            for n, tap in enumerate(taps):
                term = dot(left, tap)
                totals[n] = term if totals[n] is None else totals[n] + term
    if joined:
        totals = [totals[0][:, n * width : (n + 1) * width] for n in range(3)]
    totals = [total.reshape(height, cols, frames, width) for total in totals]
    for out in range(cols + 2):
        value = sum(
            totals[tap][:, out - 2 + tap] for tap in range(3) if 0 <= out - 2 + tap < cols
        )
        part[out] = value.reshape(height * frames, width).astype(BF16)


def straight_kernel(groups, *refs):
    pieces, (proj, straight) = refs[:groups], refs[groups:]
    rows, cols, frames, depth = pieces[0].shape
    me = lax.axis_index("grp")
    for k in range(groups):
        flat = pieces[k][...].reshape(rows * cols * frames, depth)
        direct = dot(flat, proj[...]).reshape(rows, cols, frames, proj.shape[1])
        for col in range(cols):
            straight[col, pl.ds((me ^ k) * rows, rows)] = direct[:, col]


def project_kernel(groups, *refs):
    parts, (proj, straight, odd_out, even_out, own) = refs[:groups], refs[groups:]
    extent, cells, width = parts[0].shape
    outputs = proj.shape[1]
    me = lax.axis_index("grp")
    total = None
    for k in range(groups):
        weights = proj[pl.ds(pl.multiple_of((me ^ k) * width, width), width)]
        term = dot(parts[k][...].reshape(extent * cells, width), weights)
        total = term if total is None else total + term
    total = total.reshape(extent, cells, outputs)
    cols = extent - 2
    middle = total[1 : cols + 1] + straight[...].reshape(cols, cells, outputs)
    own[0] = total[0]
    own[1 : cols + 1] = middle
    own[cols + 1] = total[cols + 1]
    left = jnp.stack([total[0], middle[0]])
    right = jnp.stack([middle[cols - 1], total[cols + 1]])
    odd = lax.axis_index("tile") % 2 == 1
    even_out[...] = jnp.where(odd, left, right).astype(BF16)
    odd_out[...] = jnp.where(odd, right, left).astype(BF16)


def middle_kernel(groups, rows, frames, odd_in, even_in, own, filters, *refs):
    outs, (block, acts, acts_odd, kept, sums) = refs[:groups], refs[groups:]
    extent, cells, depth = own.shape
    cols = extent - 2
    height = cells // frames
    me = lax.axis_index("grp")
    tile = lax.axis_index("tile")
    odd = tile % 2 == 1
    even_got = even_in[...].astype(F32)
    odd_got = odd_in[...].astype(F32)
    from_left = jnp.where(odd, even_got, odd_got)
    from_right = jnp.where(odd, odd_got, even_got)
    values = []
    for col in range(extent):
        value = own[col]
        if col < 2:
            value = value + from_left[col]
        if col >= cols:
            value = value + from_right[col - cols]
        if col == 0:
            value = jnp.where(tile == 0, 0.0, value)
        if col == extent - 1:
            value = jnp.where(tile == lax.axis_size("tile") - 1, 0.0, value)
        values.append(value.astype(BF16).astype(F32).reshape(height, frames, depth))
    nothing = jnp.zeros((1, frames, depth), F32)
    for col in range(extent):
        kept[col, 0:1] = nothing
        kept[col, 1 : height + 1] = values[col]
        kept[col, height + 1 : height + 2] = nothing
        act = activate(values[col])
        for step in range(3):
            moved = delayed(act, 2 - step)
            framed = jnp.concatenate([nothing, moved, nothing], axis=0)
            acts[step, col] = framed.reshape(cells + 2 * frames, depth).astype(BF16)
            acts_odd[step, col] = moved.reshape(cells, depth).astype(BF16)
    block[...] = (
        kept[:, pl.ds(me * rows, rows + 2)]
        .reshape(extent, (rows + 2) * frames, depth)
        .astype(BF16)
    )
    pairs = extent - 1
    total = None
    for step in range(3):
        for row in range(3):
            for side in range(2):
                if row == 1:
                    left = acts_odd[step, side : side + pairs]
                else:
                    first = row * frames
                    left = acts[step, side : side + pairs, first : first + cells]
                term = dot(left.reshape(pairs * cells, depth), filters[step, row, side])
                total = term if total is None else total + term
    lanes = total.shape[1]
    total = total.reshape(pairs, height, frames, lanes)
    empty = jnp.zeros((pairs, 1, frames, lanes), F32)
    sums[:, 0:1] = empty
    sums[:, 1 : height + 1] = total
    sums[:, height + 1 : height + 2] = empty
    half = lanes // 2
    for k in range(groups):
        chunk = sums[:, pl.ds((me ^ k) * rows, rows + 2)]
        ends = jnp.concatenate([chunk[:, rows + 1 :, :, :half], chunk[:, :1, :, half:]], axis=3)
        chunk = jnp.concatenate([ends, chunk[:, 1 : rows + 1]], axis=1)
        outs[k][...] = chunk.reshape(pairs * (rows + 1) * frames, lanes).astype(BF16)


def chunk_order(groups):
    return [0, *range(2, groups), 1]


def fine_kernel(groups, frames, *refs):
    chunks = dict(zip(chunk_order(groups), refs[:groups]))
    block, spread, proj, filters, out, acts, acts_odd, lows = refs[groups:]
    extent, cells = block.shape[:2]
    pairs, rows = extent - 1, cells // frames - 2
    width = proj.shape[1]
    tall, broad = 2 * rows, 2 * (extent - 2)
    me, last_me = lax.axis_index("grp"), lax.axis_size("grp") - 1
    tile, last_tile = lax.axis_index("tile"), lax.axis_size("tile") - 1
    total = None
    for k in range(groups):
        term = dot(chunks[k][...], spread[k])
        total = term if total is None else total + term
    total = total.reshape(pairs, rows + 1, frames, 4 * width)
    base = dot(block[...].reshape(extent * cells, block.shape[2]), proj[...])
    base = base.reshape(extent, rows + 2, frames, width)
    nothing = jnp.zeros((1, frames, width), F32)
    for col in range(broad + 2):
        pair, side = divmod(col, 2)
        upper, lower = [
            total[pair, :, :, (2 * p + side) * width : (2 * p + side + 1) * width]
            for p in range(2)
        ]
        lower = lower + base[pair + side, : rows + 1]
        upper = jnp.concatenate([upper[1:], upper[:1]], axis=0) + base[pair + side, 1:]
        woven = jnp.stack([lower, upper], axis=1)
        value = woven.reshape(tall + 2, frames, width).astype(BF16).astype(F32)
        if col == 0:
            value = jnp.where(tile == 0, 0.0, value)
        if col == broad + 1:
            value = jnp.where(tile == last_tile, 0.0, value)
        top = jnp.where(me == 0, 0.0, value[0:1])
        bottom = jnp.where(me == last_me, 0.0, value[tall + 1 : tall + 2])
        value = jnp.concatenate([top, value[1 : tall + 1], bottom], axis=0)
        lows[col] = value[1 : tall + 1]
        act = activate(value)
        for step in range(3):
            moved = delayed(act, 2 - step)
            acts[step, col] = moved.reshape((tall + 2) * frames, width).astype(BF16)
            acts_odd[step, col] = (
                moved[1 : tall + 1].reshape(tall * frames, width).astype(BF16)
            )
    span = broad + 1
    strip = tall * frames
    for p in range(2):
        sums = None
        for step in range(3):
            for near in range(2):
                row = p + near
                if row == 1:
                    pick = [acts_odd[step, side : side + span] for side in range(2)]
                else:
                    first = row * frames
                    pick = [
                        acts[step, side : side + span, first : first + strip]
                        for side in range(2)
                    ]
                left = jnp.concatenate([v.reshape(span * strip, width) for v in pick], axis=1)
                term = dot(left, filters[step, p, near])
                sums = term if sums is None else sums + term
        sums = sums.reshape(span, tall, frames, 2 * width)
        fields = []
        for col in range(2 * broad):
            pair, side = divmod(col + 1, 2)
            low = lows[pair + side]
            fields.append(sums[pair, :, :, side * width : (side + 1) * width] + low)
        field = jnp.stack(fields, axis=1)
        for row in range(tall):
            out[:, 2 * row + p] = jnp.swapaxes(field[row], 0, 1).astype(BF16)


def fold_middle_kernel(pieces, out):
    parts, n, depth = pieces.shape[0], pieces.shape[4], pieces.shape[5]

    def per_step(step, carry):
        taps = [
            [
                pieces[:, step, row, col].astype(F32).reshape(parts * n, depth)
                for col in range(3)
            ]
            for row in range(3)
        ]
        nothing = jnp.zeros((parts * n, depth), F32)
        for side in range(2):
            narrow = [
                [taps[r][0] + taps[r][1] if side == 0 else taps[r][2],
                 taps[r][0] if side == 0 else taps[r][1] + taps[r][2]]
                for r in range(3)
            ]
            for row in range(3):
                blocks = []
                for p in range(2):
                    for q in range(2):
                        if row == 1:
                            value = narrow[1][q] + narrow[2 if p == 0 else 0][q]
                        elif row == 0:
                            value = narrow[0][q] if p == 0 else nothing
                        else:
                            value = nothing if p == 0 else narrow[2][q]
                        blocks.append(value)
                out[step, row, side] = jnp.concatenate(blocks, axis=0).T.astype(BF16)
        return carry

    lax.fori_loop(0, 3, per_step, 0)


def pick_kernel(groups, stored, out, filters, arrived):
    copy = pltpu.make_async_copy(stored, filters, arrived)
    copy.start()
    me = lax.axis_index("grp")
    share = out.shape[3]
    copy.wait()
    value = filters[:, :, :, 0:share].astype(F32)
    for k in range(1, groups):
        value = jnp.where(me == k, filters[:, :, :, k * share : (k + 1) * share].astype(F32), value)
    out[...] = value.astype(BF16)


def prepare_kernel(groups, parts, filters, proj, folded, spread, plain):
    def per_step(step, carry):
        taps = [[filters[step, r, c].astype(F32) for c in range(3)] for r in range(3)]
        for p in range(2):
            for near in range(2):
                if p == 0:
                    line = taps[0] if near == 0 else [x + y for x, y in zip(taps[1], taps[2])]
                else:
                    line = [x + y for x, y in zip(taps[0], taps[1])] if near == 0 else taps[2]
                first = jnp.concatenate([line[0] + line[1], line[0]], axis=1)
                second = jnp.concatenate([line[2], line[1] + line[2]], axis=1)
                folded[step, p, near] = jnp.concatenate([first, second], axis=0).astype(BF16)
        return carry

    lax.fori_loop(0, 3, per_step, 0)
    depth, width = proj.shape
    plain[...] = proj[...].astype(F32)
    me, tile = lax.axis_index("grp"), lax.axis_index("tile")
    share = depth // (groups * parts)
    spread[...] = jnp.zeros(spread.shape, BF16)
    for k in range(groups):
        lines = []
        for s in range(parts):
            if parts == 1:
                first = (me ^ k) * share
            else:
                source = tile ^ (s // (parts // 2)) ^ (2 * (s % (parts // 2)))
                first = (source * groups + (me ^ k)) * share
            lines.append(plain[pl.ds(pl.multiple_of(first, 8), share)])
        block = jnp.concatenate(lines, axis=0).astype(BF16)
        height = parts * share
        for phase in range(4):
            spread[
                k, phase * height : (phase + 1) * height, phase * width : (phase + 1) * width
            ] = block


def exchange(values, axis, k):
    size = lax.axis_size(axis)
    return lax.ppermute(values, axis, [(i, i ^ k) for i in range(size)])


def body(latent, coarse_filters, mid_filters, fine_filters, coarse_proj, mid_proj):
    groups, tiles = lax.axis_size("grp"), lax.axis_size("tile")
    me, tile = lax.axis_index("grp"), lax.axis_index("tile")
    frames, rows, cols, depth0 = latent.shape
    depth1, depth2 = mid_proj.shape
    width0 = coarse_filters.shape[4]
    height = groups * rows
    cells = height * frames
    own_mid = mid_filters.shape[4]

    divided = own_mid % groups == 0 and (own_mid // groups) % 8 == 0
    share, shares = (own_mid // groups, tiles) if divided else (depth1 // groups, 1)
    lanes = 4 * shares * share
    arrived = [exchange(latent, "grp", k) for k in range(1, groups)]
    arrived = [with_layout_constraint(piece, Layout((0, 1, 2, 3))) for piece in arrived]
    pieces = [jnp.transpose(piece, (1, 2, 0, 3)) for piece in [latent] + arrived]

    mid_rows = jnp.transpose(mid_filters, (0, 1, 2, 4, 3))
    if divided:
        mine = call(
            functools.partial(pick_kernel, groups),
            jax.ShapeDtypeStruct((3, 3, 3, share, depth1), BF16),
            [pltpu.VMEM(mid_rows.shape, BF16), pltpu.SemaphoreType.DMA],
            6 * 10**9,
            10**6,
            mid_rows,
            stay=(0,),
        )
        near = [exchange(mine, "tile", k) for k in range(4, tiles, 2)]
        gathered = jnp.stack([mine, *near])
    else:
        every = lax.all_gather(mid_rows, "tile", axis=3, tiled=True)
        mine = lax.dynamic_slice_in_dim(every, me * share, share, axis=3)[None]

    part = call(
        functools.partial(coarse_kernel, groups),
        jax.ShapeDtypeStruct((cols + 2, cells, width0), BF16),
        [pltpu.VMEM((3, height + 2, cols * frames, depth0), BF16)],
        5 * 10**8,
        10**5,
        *pieces,
        coarse_filters,
    )
    straight = call(
        functools.partial(straight_kernel, groups),
        jax.ShapeDtypeStruct((cols, height, frames, depth1), F32),
        [],
        2 * cells * cols * depth0 * depth1,
        10**6,
        *pieces,
        coarse_proj,
    )
    parts = [part] + [exchange(part, "grp", k) for k in range(1, groups)]
    if divided:
        later, _ = lax.optimization_barrier((mine, part))
        beyond = exchange(later, "tile", 2)
    odd_out, even_out, own = call(
        functools.partial(project_kernel, groups),
        (
            jax.ShapeDtypeStruct((2, cells, depth1), BF16),
            jax.ShapeDtypeStruct((2, cells, depth1), BF16),
            jax.ShapeDtypeStruct((cols + 2, cells, depth1), F32),
        ),
        [],
        2 * cells * (cols + 2) * depth0 * depth1,
        2 * 10**6,
        *parts,
        coarse_proj,
        straight,
    )
    odd_pairs = [(i, i + 1) for i in range(1, tiles - 1, 2)]
    odd_in = lax.ppermute(odd_out, "tile", odd_pairs + [(j, i) for i, j in odd_pairs])
    even_in = exchange(even_out, "tile", 1)
    if divided:
        gathered, beyond, _ = lax.optimization_barrier((gathered, beyond, own))
        mine = jnp.concatenate([gathered[:1], beyond[None], gathered[1:]])
        mine = jnp.concatenate([mine, exchange(mine, "tile", 1)])
    mid_folded = call(
        fold_middle_kernel,
        jax.ShapeDtypeStruct((3, 3, 2, depth1, lanes), BF16),
        [],
        10**6,
        4 * 10**6,
        mine,
    )
    local = (rows + 2) * frames
    *chunks, block = call(
        functools.partial(middle_kernel, groups, rows, frames),
        tuple(
            jax.ShapeDtypeStruct(((cols + 1) * (rows + 1) * frames, lanes), BF16)
            for _ in range(groups)
        )
        + (jax.ShapeDtypeStruct((cols + 2, local, depth1), BF16),),
        [
            pltpu.VMEM((3, cols + 2, cells + 2 * frames, depth1), BF16),
            pltpu.VMEM((3, cols + 2, cells, depth1), BF16),
            pltpu.VMEM((cols + 2, height + 2, frames, depth1), F32),
            pltpu.VMEM((cols + 1, height + 2, frames, lanes), F32),
        ],
        2 * 18 * (cols + 1) * cells * depth1 * lanes,
        5 * 10**6,
        odd_in,
        even_in,
        own,
        mid_folded,
    )
    chunks = [chunks[0]] + [exchange(chunks[k], "grp", k) for k in range(1, groups)]
    fine_folded, spread = call(
        functools.partial(prepare_kernel, groups, shares),
        (
            jax.ShapeDtypeStruct((3, 2, 2, 2 * depth2, 2 * depth2), BF16),
            jax.ShapeDtypeStruct((groups, lanes, 4 * depth2), BF16),
        ),
        [pltpu.VMEM((depth1, depth2), F32)],
        10**6,
        4 * 10**6,
        fine_filters,
        mid_proj,
    )
    tall, broad = 2 * rows, 2 * cols
    return call(
        functools.partial(fine_kernel, groups, frames),
        jax.ShapeDtypeStruct((frames, 2 * tall, 2 * broad, depth2), BF16),
        [
            pltpu.VMEM((3, broad + 2, (tall + 2) * frames, depth2), BF16),
            pltpu.VMEM((3, broad + 2, tall * frames, depth2), BF16),
            pltpu.VMEM((broad + 2, tall, frames, depth2), F32),
        ],
        2 * 24 * (broad + 1) * tall * frames * depth2 * 2 * depth2,
        3 * 10**6,
        *[chunks[k] for k in chunk_order(groups)],
        block,
        spread,
        mid_proj,
        fine_folded,
    )


def solution(mesh):
    in_specs = (
        P(None, "grp", "tile", None),
        P(None, None, None, None, "grp"),
        P(None, None, None, None, "tile"),
        P(),
        P(),
        P(),
    )
    out_specs = P(None, "grp", "tile", None)
    return jax.shard_map(body, mesh=mesh, in_specs=in_specs, out_specs=out_specs, check_vma=False)
```

```python
import functools

import jax
import jax.numpy as jnp
from jax import lax
from jax.experimental import pallas as pl
from jax.experimental.layout import Layout, with_layout_constraint
from jax.experimental.pallas import tpu as pltpu
from jax.sharding import PartitionSpec as P

VMEM = pl.BlockSpec(memory_space=pltpu.VMEM)
FAR = pl.BlockSpec(memory_space=pltpu.HBM)
F32 = jnp.float32
BF16 = jnp.bfloat16


def call(kernel, outs, scratch, flops, nbytes, *args, stay=()):
    args = [
        pltpu.with_memory_space_constraint(arg, pltpu.HBM) if n in stay else arg
        for n, arg in enumerate(args)
    ]
    return pl.pallas_call(
        kernel,
        out_shape=outs,
        in_specs=[FAR if n in stay else VMEM for n in range(len(args))],
        out_specs=jax.tree.map(lambda _: VMEM, outs),
        scratch_shapes=scratch,
        compiler_params=pltpu.CompilerParams(vmem_limit_bytes=40 << 20),
        cost_estimate=pl.CostEstimate(flops=flops, bytes_accessed=nbytes, transcendentals=0),
    )(*args)


def dot(left, right):
    return jnp.dot(left, right, preferred_element_type=F32)


def activate(values):
    scaled = values * lax.rsqrt(jnp.mean(values * values, axis=-1, keepdims=True) + 1e-06)
    return scaled / (1.0 + jnp.exp(-scaled))


def delayed(values, steps):
    if steps == 0:
        return values
    axis = values.ndim - 2
    frame = lax.broadcasted_iota(jnp.int32, values.shape, axis)
    return jnp.where(frame >= steps, pltpu.roll(values, steps, axis), 0.0)


def coarse_kernel(groups, *refs):
    pieces, (filters, part, shifted) = refs[:groups], refs[groups:]
    rows, cols, frames, depth = pieces[0].shape
    width = filters.shape[4]
    height = groups * rows
    me = lax.axis_index("grp")
    edge = jnp.zeros((1, cols * frames, depth), BF16)
    for step in range(3):
        shifted[step, 0:1] = edge
        shifted[step, height + 1 : height + 2] = edge
    for k in range(groups):
        at = (me ^ k) * rows
        raw = pieces[k][...]
        act = activate(raw.astype(F32))
        for step in range(3):
            moved = delayed(act, 2 - step).reshape(rows, cols * frames, depth)
            shifted[step, pl.ds(at + 1, rows)] = moved.astype(BF16)
    joined = width % 128 == 0
    totals = [None] * (1 if joined else 3)
    for step in range(3):
        for row in range(3):
            left = shifted[step, row : row + height].reshape(height * cols * frames, depth)
            taps = [filters[step, row, col] for col in range(3)]
            if joined:
                taps = [jnp.concatenate(taps, axis=1)]
            for n, tap in enumerate(taps):
                term = dot(left, tap)
                totals[n] = term if totals[n] is None else totals[n] + term
    if joined:
        totals = [totals[0][:, n * width : (n + 1) * width] for n in range(3)]
    totals = [total.reshape(height, cols, frames, width) for total in totals]
    for out in range(cols + 2):
        value = sum(
            totals[tap][:, out - 2 + tap] for tap in range(3) if 0 <= out - 2 + tap < cols
        )
        part[out] = value.reshape(height * frames, width).astype(BF16)


def straight_kernel(groups, *refs):
    pieces, (proj, straight) = refs[:groups], refs[groups:]
    rows, cols, frames, depth = pieces[0].shape
    me = lax.axis_index("grp")
    for k in range(groups):
        flat = pieces[k][...].reshape(rows * cols * frames, depth)
        direct = dot(flat, proj[...]).reshape(rows, cols, frames, proj.shape[1])
        for col in range(cols):
            straight[col, pl.ds((me ^ k) * rows, rows)] = direct[:, col]


def project_kernel(groups, *refs):
    parts, (proj, straight), (odd_out, even_out, own) = (
        refs[:groups], refs[groups : groups + 2], refs[-3:],
    )
    extent, cells, width = parts[0].shape
    outputs = proj.shape[1]
    me = lax.axis_index("grp")
    total = None
    for k in range(groups):
        weights = proj[pl.ds(pl.multiple_of((me ^ k) * width, width), width)]
        term = dot(parts[k][...].reshape(extent * cells, width), weights)
        total = term if total is None else total + term
    total = total.reshape(extent, cells, outputs)
    cols = extent - 2
    middle = total[1 : cols + 1] + straight[...].reshape(cols, cells, outputs)
    own[0] = total[0]
    own[1 : cols + 1] = middle
    own[cols + 1] = total[cols + 1]
    left = jnp.stack([total[0], middle[0]])
    right = jnp.stack([middle[cols - 1], total[cols + 1]])
    odd = lax.axis_index("tile") % 2 == 1
    even_out[...] = jnp.where(odd, left, right).astype(BF16)
    odd_out[...] = jnp.where(odd, right, left).astype(BF16)


def middle_kernel(groups, rows, frames, odd_in, even_in, own, filters, *refs):
    outs, (block, acts, acts_odd, kept, sums) = refs[:groups], refs[groups:]
    extent, cells, depth = own.shape
    cols = extent - 2
    height = cells // frames
    me = lax.axis_index("grp")
    tile = lax.axis_index("tile")
    odd = tile % 2 == 1
    even_got = even_in[...].astype(F32)
    odd_got = odd_in[...].astype(F32)
    from_left = jnp.where(odd, even_got, odd_got)
    from_right = jnp.where(odd, odd_got, even_got)
    values = []
    for col in range(extent):
        value = own[col]
        if col < 2:
            value = value + from_left[col]
        if col >= cols:
            value = value + from_right[col - cols]
        if col == 0:
            value = jnp.where(tile == 0, 0.0, value)
        if col == extent - 1:
            value = jnp.where(tile == lax.axis_size("tile") - 1, 0.0, value)
        values.append(value.astype(BF16).astype(F32).reshape(height, frames, depth))
    nothing = jnp.zeros((1, frames, depth), F32)
    for col in range(extent):
        kept[col, 0:1] = nothing
        kept[col, 1 : height + 1] = values[col]
        kept[col, height + 1 : height + 2] = nothing
        act = activate(values[col])
        for step in range(3):
            moved = delayed(act, 2 - step)
            framed = jnp.concatenate([nothing, moved, nothing], axis=0)
            acts[step, col] = framed.reshape(cells + 2 * frames, depth).astype(BF16)
            acts_odd[step, col] = moved.reshape(cells, depth).astype(BF16)
    block[...] = (
        kept[:, pl.ds(me * rows, rows + 2)]
        .reshape(extent, (rows + 2) * frames, depth)
        .astype(BF16)
    )
    pairs = extent - 1
    total = None
    for step in range(3):
        for row in range(3):
            for side in range(2):
                if row == 1:
                    left = acts_odd[step, side : side + pairs]
                else:
                    first = row * frames
                    left = acts[step, side : side + pairs, first : first + cells]
                term = dot(left.reshape(pairs * cells, depth), filters[step, row, side])
                total = term if total is None else total + term
    lanes = total.shape[1]
    total = total.reshape(pairs, height, frames, lanes)
    empty = jnp.zeros((pairs, 1, frames, lanes), F32)
    sums[:, 0:1] = empty
    sums[:, 1 : height + 1] = total
    sums[:, height + 1 : height + 2] = empty
    half = lanes // 2
    for k in range(groups):
        chunk = sums[:, pl.ds((me ^ k) * rows, rows + 2)]
        ends = jnp.concatenate([chunk[:, rows + 1 :, :, :half], chunk[:, :1, :, half:]], axis=3)
        chunk = jnp.concatenate([ends, chunk[:, 1 : rows + 1]], axis=1)
        outs[k][...] = chunk.reshape(pairs * (rows + 1) * frames, lanes).astype(BF16)


def chunk_order(groups):
    return [0, *range(2, groups), 1]


def fine_kernel(groups, frames, *refs):
    chunks = dict(zip(chunk_order(groups), refs[:groups]))
    block, spread, proj, filters, out, acts, acts_odd, lows = refs[groups:]
    extent, cells = block.shape[:2]
    pairs, rows = extent - 1, cells // frames - 2
    width = proj.shape[1]
    tall, broad = 2 * rows, 2 * (extent - 2)
    me, last_me = lax.axis_index("grp"), lax.axis_size("grp") - 1
    tile, last_tile = lax.axis_index("tile"), lax.axis_size("tile") - 1
    total = None
    for k in range(groups):
        term = dot(chunks[k][...], spread[k])
        total = term if total is None else total + term
    total = total.reshape(pairs, rows + 1, frames, 4 * width)
    base = dot(block[...].reshape(extent * cells, block.shape[2]), proj[...])
    base = base.reshape(extent, rows + 2, frames, width)
    nothing = jnp.zeros((1, frames, width), F32)
    for col in range(broad + 2):
        pair, side = divmod(col, 2)
        upper, lower = [
            total[pair, :, :, (2 * p + side) * width : (2 * p + side + 1) * width]
            for p in range(2)
        ]
        lower = lower + base[pair + side, : rows + 1]
        upper = jnp.concatenate([upper[1:], upper[:1]], axis=0) + base[pair + side, 1:]
        woven = jnp.stack([lower, upper], axis=1)
        value = woven.reshape(tall + 2, frames, width).astype(BF16).astype(F32)
        if col == 0:
            value = jnp.where(tile == 0, 0.0, value)
        if col == broad + 1:
            value = jnp.where(tile == last_tile, 0.0, value)
        top = jnp.where(me == 0, 0.0, value[0:1])
        bottom = jnp.where(me == last_me, 0.0, value[tall + 1 : tall + 2])
        value = jnp.concatenate([top, value[1 : tall + 1], bottom], axis=0)
        lows[col] = value[1 : tall + 1]
        act = activate(value)
        for step in range(3):
            moved = delayed(act, 2 - step)
            acts[step, col] = moved.reshape((tall + 2) * frames, width).astype(BF16)
            acts_odd[step, col] = (
                moved[1 : tall + 1].reshape(tall * frames, width).astype(BF16)
            )
    span = broad + 1
    strip = tall * frames
    for p in range(2):
        sums = None
        for step in range(3):
            for near in range(2):
                row = p + near
                if row == 1:
                    pick = [acts_odd[step, side : side + span] for side in range(2)]
                else:
                    first = row * frames
                    pick = [
                        acts[step, side : side + span, first : first + strip]
                        for side in range(2)
                    ]
                left = jnp.concatenate([v.reshape(span * strip, width) for v in pick], axis=1)
                term = dot(left, filters[step, p, near])
                sums = term if sums is None else sums + term
        sums = sums.reshape(span, tall, frames, 2 * width)
        fields = []
        for col in range(2 * broad):
            pair, side = divmod(col + 1, 2)
            low = lows[pair + side]
            fields.append(sums[pair, :, :, side * width : (side + 1) * width] + low)
        field = jnp.stack(fields, axis=1)
        for row in range(tall):
            out[:, 2 * row + p] = jnp.swapaxes(field[row], 0, 1).astype(BF16)


def fold_middle_kernel(pieces, out):
    parts, n, depth = pieces.shape[0], pieces.shape[4], pieces.shape[5]

    def per_step(step, carry):
        taps = [
            [
                pieces[:, step, row, col].astype(F32).reshape(parts * n, depth)
                for col in range(3)
            ]
            for row in range(3)
        ]
        nothing = jnp.zeros((parts * n, depth), F32)
        for side in range(2):
            narrow = [
                [taps[r][0] + taps[r][1] if side == 0 else taps[r][2],
                 taps[r][0] if side == 0 else taps[r][1] + taps[r][2]]
                for r in range(3)
            ]
            for row in range(3):
                blocks = []
                for p in range(2):
                    for q in range(2):
                        if row == 1:
                            value = narrow[1][q] + narrow[2 if p == 0 else 0][q]
                        elif row == 0:
                            value = narrow[0][q] if p == 0 else nothing
                        else:
                            value = nothing if p == 0 else narrow[2][q]
                        blocks.append(value)
                out[step, row, side] = jnp.concatenate(blocks, axis=0).T.astype(BF16)
        return carry

    lax.fori_loop(0, 3, per_step, 0)


def pick_kernel(groups, stored, out, filters, arrived):
    copy = pltpu.make_async_copy(stored, filters, arrived)
    copy.start()
    me = lax.axis_index("grp")
    share = out.shape[3]
    copy.wait()
    value = filters[:, :, :, 0:share].astype(F32)
    for k in range(1, groups):
        value = jnp.where(me == k, filters[:, :, :, k * share : (k + 1) * share].astype(F32), value)
    out[...] = value.astype(BF16)


def prepare_kernel(groups, parts, filters, proj, folded, spread, plain):
    def per_step(step, carry):
        taps = [[filters[step, r, c].astype(F32) for c in range(3)] for r in range(3)]
        for p in range(2):
            for near in range(2):
                if p == 0:
                    line = taps[0] if near == 0 else [x + y for x, y in zip(taps[1], taps[2])]
                else:
                    line = [x + y for x, y in zip(taps[0], taps[1])] if near == 0 else taps[2]
                first = jnp.concatenate([line[0] + line[1], line[0]], axis=1)
                second = jnp.concatenate([line[2], line[1] + line[2]], axis=1)
                folded[step, p, near] = jnp.concatenate([first, second], axis=0).astype(BF16)
        return carry

    lax.fori_loop(0, 3, per_step, 0)
    depth, width = proj.shape
    plain[...] = proj[...].astype(F32)
    me, tile = lax.axis_index("grp"), lax.axis_index("tile")
    share = depth // (groups * parts)
    spread[...] = jnp.zeros(spread.shape, BF16)
    for k in range(groups):
        lines = []
        for s in range(parts):
            if parts == 1:
                first = (me ^ k) * share
            else:
                source = tile ^ (s // (parts // 2)) ^ (2 * (s % (parts // 2)))
                first = (source * groups + (me ^ k)) * share
            lines.append(plain[pl.ds(pl.multiple_of(first, 8), share)])
        block = jnp.concatenate(lines, axis=0).astype(BF16)
        height = parts * share
        for phase in range(4):
            spread[
                k, phase * height : (phase + 1) * height, phase * width : (phase + 1) * width
            ] = block


def exchange(values, axis, k):
    size = lax.axis_size(axis)
    return lax.ppermute(values, axis, [(i, i ^ k) for i in range(size)])


def body(latent, coarse_filters, mid_filters, fine_filters, coarse_proj, mid_proj):
    groups, tiles = lax.axis_size("grp"), lax.axis_size("tile")
    me, tile = lax.axis_index("grp"), lax.axis_index("tile")
    frames, rows, cols, depth0 = latent.shape
    depth1, depth2 = mid_proj.shape
    width0 = coarse_filters.shape[4]
    height = groups * rows
    cells = height * frames
    own_mid = mid_filters.shape[4]

    early = []
    divided = own_mid % groups == 0 and (own_mid // groups) % 8 == 0
    share, shares = (own_mid // groups, tiles) if divided else (depth1 // groups, 1)
    lanes = 4 * shares * share
    arrived = [exchange(latent, "grp", k) for k in range(1, groups)]
    arrived = [with_layout_constraint(piece, Layout((0, 1, 2, 3))) for piece in arrived]
    pieces = [jnp.transpose(piece, (1, 2, 0, 3)) for piece in [latent] + arrived]

    mid_rows = jnp.transpose(mid_filters, (0, 1, 2, 4, 3))
    if divided:
        mine = call(
            functools.partial(pick_kernel, groups),
            jax.ShapeDtypeStruct((3, 3, 3, share, depth1), BF16),
            [pltpu.VMEM(mid_rows.shape, BF16), pltpu.SemaphoreType.DMA],
            6 * 10**9,
            10**6,
            mid_rows,
            stay=(0,),
        )
        near = [exchange(mine, "tile", k) for k in range(4, tiles, 2)]
        gathered = jnp.stack([mine, *near])
        early = [exchange(gathered, "tile", 1)]
    else:
        every = lax.all_gather(mid_rows, "tile", axis=3, tiled=True)
        mine = lax.dynamic_slice_in_dim(every, me * share, share, axis=3)[None]

    part = call(
        functools.partial(coarse_kernel, groups),
        jax.ShapeDtypeStruct((cols + 2, cells, width0), BF16),
        [pltpu.VMEM((3, height + 2, cols * frames, depth0), BF16)],
        2 * 10**9,
        10**5,
        *pieces,
        coarse_filters,
    )
    straight = call(
        functools.partial(straight_kernel, groups),
        jax.ShapeDtypeStruct((cols, height, frames, depth1), F32),
        [],
        5 * 10**9,
        10**6,
        *pieces,
        coarse_proj,
    )
    parts = [part] + [exchange(part, "grp", k) for k in range(1, groups)]
    if divided:
        later, _ = lax.optimization_barrier((mine, part))
        beyond = exchange(later, "tile", 2)
    odd_out, even_out, own = call(
        functools.partial(project_kernel, groups),
        (
            jax.ShapeDtypeStruct((2, cells, depth1), BF16),
            jax.ShapeDtypeStruct((2, cells, depth1), BF16),
            jax.ShapeDtypeStruct((cols + 2, cells, depth1), F32),
        ),
        [],
        2 * cells * (cols + 2) * depth0 * depth1,
        2 * 10**6,
        *parts,
        coarse_proj,
        straight,
        *early,
    )
    odd_pairs = [(i, i + 1) for i in range(1, tiles - 1, 2)]
    odd_in = lax.ppermute(odd_out, "tile", odd_pairs + [(j, i) for i, j in odd_pairs])
    even_in = exchange(even_out, "tile", 1)
    if divided:
        gathered, beyond, _ = lax.optimization_barrier((gathered, beyond, own))
        beyond = beyond[None]
        got = early[0]
        mine = jnp.concatenate(
            [gathered[:1], beyond, gathered[1:], got[:1], exchange(beyond, "tile", 1), got[1:]]
        )
    mid_folded = call(
        fold_middle_kernel,
        jax.ShapeDtypeStruct((3, 3, 2, depth1, lanes), BF16),
        [],
        10**6,
        4 * 10**6,
        mine,
    )
    local = (rows + 2) * frames
    *chunks, block = call(
        functools.partial(middle_kernel, groups, rows, frames),
        tuple(
            jax.ShapeDtypeStruct(((cols + 1) * (rows + 1) * frames, lanes), BF16)
            for _ in range(groups)
        )
        + (jax.ShapeDtypeStruct((cols + 2, local, depth1), BF16),),
        [
            pltpu.VMEM((3, cols + 2, cells + 2 * frames, depth1), BF16),
            pltpu.VMEM((3, cols + 2, cells, depth1), BF16),
            pltpu.VMEM((cols + 2, height + 2, frames, depth1), F32),
            pltpu.VMEM((cols + 1, height + 2, frames, lanes), F32),
        ],
        2 * 18 * (cols + 1) * cells * depth1 * lanes,
        5 * 10**6,
        odd_in,
        even_in,
        own,
        mid_folded,
    )
    chunks = [chunks[0]] + [exchange(chunks[k], "grp", k) for k in range(1, groups)]
    fine_folded, spread = call(
        functools.partial(prepare_kernel, groups, shares),
        (
            jax.ShapeDtypeStruct((3, 2, 2, 2 * depth2, 2 * depth2), BF16),
            jax.ShapeDtypeStruct((groups, lanes, 4 * depth2), BF16),
        ),
        [pltpu.VMEM((depth1, depth2), F32)],
        10**6,
        4 * 10**6,
        fine_filters,
        mid_proj,
    )
    tall, broad = 2 * rows, 2 * cols
    return call(
        functools.partial(fine_kernel, groups, frames),
        jax.ShapeDtypeStruct((frames, 2 * tall, 2 * broad, depth2), BF16),
        [
            pltpu.VMEM((3, broad + 2, (tall + 2) * frames, depth2), BF16),
            pltpu.VMEM((3, broad + 2, tall * frames, depth2), BF16),
            pltpu.VMEM((broad + 2, tall, frames, depth2), F32),
        ],
        2 * 24 * (broad + 1) * tall * frames * depth2 * 2 * depth2,
        3 * 10**6,
        *[chunks[k] for k in chunk_order(groups)],
        block,
        spread,
        mid_proj,
        fine_folded,
    )


def solution(mesh):
    in_specs = (
        P(None, "grp", "tile", None),
        P(None, None, None, None, "grp"),
        P(None, None, None, None, "tile"),
        P(),
        P(),
        P(),
    )
    out_specs = P(None, "grp", "tile", None)
    return jax.shard_map(body, mesh=mesh, in_specs=in_specs, out_specs=out_specs, check_vma=False)
```

```python
import functools

import jax
import jax.numpy as jnp
from jax import lax
from jax.experimental import pallas as pl
from jax.experimental.layout import Layout, with_layout_constraint
from jax.experimental.pallas import tpu as pltpu
from jax.sharding import PartitionSpec as P

VMEM = pl.BlockSpec(memory_space=pltpu.VMEM)
FAR = pl.BlockSpec(memory_space=pltpu.HBM)
F32 = jnp.float32
BF16 = jnp.bfloat16


def call(kernel, outs, scratch, flops, nbytes, *args, stay=()):
    args = [
        pltpu.with_memory_space_constraint(arg, pltpu.HBM) if n in stay else arg
        for n, arg in enumerate(args)
    ]
    return pl.pallas_call(
        kernel,
        out_shape=outs,
        in_specs=[FAR if n in stay else VMEM for n in range(len(args))],
        out_specs=jax.tree.map(lambda _: VMEM, outs),
        scratch_shapes=scratch,
        compiler_params=pltpu.CompilerParams(vmem_limit_bytes=40 << 20),
        cost_estimate=pl.CostEstimate(flops=flops, bytes_accessed=nbytes, transcendentals=0),
    )(*args)


def dot(left, right):
    return jnp.dot(left, right, preferred_element_type=F32)


def activate(values):
    scaled = values * lax.rsqrt(jnp.mean(values * values, axis=-1, keepdims=True) + 1e-06)
    return scaled / (1.0 + jnp.exp(-scaled))


def delayed(values, steps):
    if steps == 0:
        return values
    axis = values.ndim - 2
    frame = lax.broadcasted_iota(jnp.int32, values.shape, axis)
    return jnp.where(frame >= steps, pltpu.roll(values, steps, axis), 0.0)


def coarse_kernel(groups, *refs):
    pieces, (filters, part, shifted) = refs[:groups], refs[groups:]
    rows, cols, frames, depth = pieces[0].shape
    width = filters.shape[4]
    height = groups * rows
    me = lax.axis_index("grp")
    edge = jnp.zeros((1, cols * frames, depth), BF16)
    for step in range(3):
        shifted[step, 0:1] = edge
        shifted[step, height + 1 : height + 2] = edge
    for k in range(groups):
        at = (me ^ k) * rows
        raw = pieces[k][...]
        act = activate(raw.astype(F32))
        for step in range(3):
            moved = delayed(act, 2 - step).reshape(rows, cols * frames, depth)
            shifted[step, pl.ds(at + 1, rows)] = moved.astype(BF16)
    if width % 128 == 0:
        total = None
        for step in range(3):
            left = shifted[step, 1 : height + 1].reshape(height * cols * frames, depth)
            taps = [filters[step, row, col] for row in range(3) for col in range(3)]
            term = dot(left, jnp.concatenate(taps, axis=1))
            total = term if total is None else total + term
        total = total.reshape(height, cols * frames, 9 * width)
        above, level, below = [total[:, :, 3 * n * width : 3 * (n + 1) * width] for n in range(3)]
        nothing = jnp.zeros((1, cols * frames, 3 * width), F32)
        total = (
            level
            + jnp.concatenate([nothing, above[:-1]], axis=0)
            + jnp.concatenate([below[1:], nothing], axis=0)
        )
        totals = [total[:, :, n * width : (n + 1) * width] for n in range(3)]
    else:
        totals = [None] * 3
        for step in range(3):
            for row in range(3):
                left = shifted[step, row : row + height].reshape(height * cols * frames, depth)
                for col in range(3):
                    term = dot(left, filters[step, row, col])
                    totals[col] = term if totals[col] is None else totals[col] + term
    totals = [total.reshape(height, cols, frames, width) for total in totals]
    for out in range(cols + 2):
        value = sum(
            totals[tap][:, out - 2 + tap] for tap in range(3) if 0 <= out - 2 + tap < cols
        )
        part[out] = value.reshape(height * frames, width).astype(BF16)


def straight_kernel(groups, *refs):
    pieces, (proj, straight) = refs[:groups], refs[groups:]
    rows, cols, frames, depth = pieces[0].shape
    me = lax.axis_index("grp")
    for k in range(groups):
        flat = pieces[k][...].reshape(rows * cols * frames, depth)
        direct = dot(flat, proj[...]).reshape(rows, cols, frames, proj.shape[1])
        for col in range(cols):
            straight[col, pl.ds((me ^ k) * rows, rows)] = direct[:, col]


def project_kernel(groups, *refs):
    parts, (proj, straight), (odd_out, even_out, own) = (
        refs[:groups], refs[groups : groups + 2], refs[-3:],
    )
    extent, cells, width = parts[0].shape
    outputs = proj.shape[1]
    me = lax.axis_index("grp")
    total = None
    for k in range(groups):
        weights = proj[pl.ds(pl.multiple_of((me ^ k) * width, width), width)]
        term = dot(parts[k][...].reshape(extent * cells, width), weights)
        total = term if total is None else total + term
    total = total.reshape(extent, cells, outputs)
    cols = extent - 2
    middle = total[1 : cols + 1] + straight[...].reshape(cols, cells, outputs)
    own[0] = total[0]
    own[1 : cols + 1] = middle
    own[cols + 1] = total[cols + 1]
    left = jnp.stack([total[0], middle[0]])
    right = jnp.stack([middle[cols - 1], total[cols + 1]])
    odd = lax.axis_index("tile") % 2 == 1
    even_out[...] = jnp.where(odd, left, right).astype(BF16)
    odd_out[...] = jnp.where(odd, right, left).astype(BF16)


def middle_kernel(groups, rows, frames, odd_in, even_in, own, filters, *refs):
    outs, (block, acts, acts_odd, kept, sums) = refs[:groups], refs[groups:]
    extent, cells, depth = own.shape
    cols = extent - 2
    height = cells // frames
    me = lax.axis_index("grp")
    tile = lax.axis_index("tile")
    odd = tile % 2 == 1
    even_got = even_in[...].astype(F32)
    odd_got = odd_in[...].astype(F32)
    from_left = jnp.where(odd, even_got, odd_got)
    from_right = jnp.where(odd, odd_got, even_got)
    values = []
    for col in range(extent):
        value = own[col]
        if col < 2:
            value = value + from_left[col]
        if col >= cols:
            value = value + from_right[col - cols]
        if col == 0:
            value = jnp.where(tile == 0, 0.0, value)
        if col == extent - 1:
            value = jnp.where(tile == lax.axis_size("tile") - 1, 0.0, value)
        values.append(value.astype(BF16).astype(F32).reshape(height, frames, depth))
    nothing = jnp.zeros((1, frames, depth), F32)
    for col in range(extent):
        kept[col, 0:1] = nothing
        kept[col, 1 : height + 1] = values[col]
        kept[col, height + 1 : height + 2] = nothing
        act = activate(values[col])
        for step in range(3):
            moved = delayed(act, 2 - step)
            framed = jnp.concatenate([nothing, moved, nothing], axis=0)
            acts[step, col] = framed.reshape(cells + 2 * frames, depth).astype(BF16)
            acts_odd[step, col] = moved.reshape(cells, depth).astype(BF16)
    block[...] = (
        kept[:, pl.ds(me * rows, rows + 2)]
        .reshape(extent, (rows + 2) * frames, depth)
        .astype(BF16)
    )
    pairs = extent - 1
    total = None
    for step in range(3):
        for row in range(3):
            for side in range(2):
                if row == 1:
                    left = acts_odd[step, side : side + pairs]
                else:
                    first = row * frames
                    left = acts[step, side : side + pairs, first : first + cells]
                term = dot(left.reshape(pairs * cells, depth), filters[step, row, side])
                total = term if total is None else total + term
    lanes = total.shape[1]
    total = total.reshape(pairs, height, frames, lanes)
    empty = jnp.zeros((pairs, 1, frames, lanes), F32)
    sums[:, 0:1] = empty
    sums[:, 1 : height + 1] = total
    sums[:, height + 1 : height + 2] = empty
    half = lanes // 2
    for k in range(groups):
        chunk = sums[:, pl.ds((me ^ k) * rows, rows + 2)]
        ends = jnp.concatenate([chunk[:, rows + 1 :, :, :half], chunk[:, :1, :, half:]], axis=3)
        chunk = jnp.concatenate([ends, chunk[:, 1 : rows + 1]], axis=1)
        outs[k][...] = chunk.reshape(pairs * (rows + 1) * frames, lanes).astype(BF16)


def chunk_order(groups):
    return [0, *range(2, groups), 1]


def fine_kernel(groups, frames, *refs):
    chunks = dict(zip(chunk_order(groups), refs[:groups]))
    block, spread, proj, filters, out, acts, acts_odd, lows = refs[groups:]
    extent, cells = block.shape[:2]
    pairs, rows = extent - 1, cells // frames - 2
    width = proj.shape[1]
    tall, broad = 2 * rows, 2 * (extent - 2)
    me, last_me = lax.axis_index("grp"), lax.axis_size("grp") - 1
    tile, last_tile = lax.axis_index("tile"), lax.axis_size("tile") - 1
    total = None
    for k in range(groups):
        term = dot(chunks[k][...], spread[k])
        total = term if total is None else total + term
    total = total.reshape(pairs, rows + 1, frames, 4 * width)
    base = dot(block[...].reshape(extent * cells, block.shape[2]), proj[...])
    base = base.reshape(extent, rows + 2, frames, width)
    nothing = jnp.zeros((1, frames, width), F32)
    for col in range(broad + 2):
        pair, side = divmod(col, 2)
        upper, lower = [
            total[pair, :, :, (2 * p + side) * width : (2 * p + side + 1) * width]
            for p in range(2)
        ]
        lower = lower + base[pair + side, : rows + 1]
        upper = jnp.concatenate([upper[1:], upper[:1]], axis=0) + base[pair + side, 1:]
        woven = jnp.stack([lower, upper], axis=1)
        value = woven.reshape(tall + 2, frames, width).astype(BF16).astype(F32)
        if col == 0:
            value = jnp.where(tile == 0, 0.0, value)
        if col == broad + 1:
            value = jnp.where(tile == last_tile, 0.0, value)
        top = jnp.where(me == 0, 0.0, value[0:1])
        bottom = jnp.where(me == last_me, 0.0, value[tall + 1 : tall + 2])
        value = jnp.concatenate([top, value[1 : tall + 1], bottom], axis=0)
        lows[col] = value[1 : tall + 1]
        act = activate(value)
        for step in range(3):
            moved = delayed(act, 2 - step)
            acts[step, col] = moved.reshape((tall + 2) * frames, width).astype(BF16)
            acts_odd[step, col] = (
                moved[1 : tall + 1].reshape(tall * frames, width).astype(BF16)
            )
    span = broad + 1
    strip = tall * frames
    for p in range(2):
        sums = None
        for step in range(3):
            for near in range(2):
                row = p + near
                if row == 1:
                    pick = [acts_odd[step, side : side + span] for side in range(2)]
                else:
                    first = row * frames
                    pick = [
                        acts[step, side : side + span, first : first + strip]
                        for side in range(2)
                    ]
                left = jnp.concatenate([v.reshape(span * strip, width) for v in pick], axis=1)
                term = dot(left, filters[step, p, near])
                sums = term if sums is None else sums + term
        sums = sums.reshape(span, tall, frames, 2 * width)
        fields = []
        for col in range(2 * broad):
            pair, side = divmod(col + 1, 2)
            low = lows[pair + side]
            fields.append(sums[pair, :, :, side * width : (side + 1) * width] + low)
        field = jnp.stack(fields, axis=1)
        for row in range(tall):
            out[:, 2 * row + p] = jnp.swapaxes(field[row], 0, 1).astype(BF16)


def fold_middle_kernel(pieces, out):
    parts, n, depth = pieces.shape[0], pieces.shape[4], pieces.shape[5]

    def per_step(step, carry):
        taps = [
            [
                pieces[:, step, row, col].astype(F32).reshape(parts * n, depth)
                for col in range(3)
            ]
            for row in range(3)
        ]
        nothing = jnp.zeros((parts * n, depth), F32)
        for side in range(2):
            narrow = [
                [taps[r][0] + taps[r][1] if side == 0 else taps[r][2],
                 taps[r][0] if side == 0 else taps[r][1] + taps[r][2]]
                for r in range(3)
            ]
            for row in range(3):
                blocks = []
                for p in range(2):
                    for q in range(2):
                        if row == 1:
                            value = narrow[1][q] + narrow[2 if p == 0 else 0][q]
                        elif row == 0:
                            value = narrow[0][q] if p == 0 else nothing
                        else:
                            value = nothing if p == 0 else narrow[2][q]
                        blocks.append(value)
                out[step, row, side] = jnp.concatenate(blocks, axis=0).T.astype(BF16)
        return carry

    lax.fori_loop(0, 3, per_step, 0)


def pick_kernel(groups, stored, out, filters, arrived):
    copy = pltpu.make_async_copy(stored, filters, arrived)
    copy.start()
    me = lax.axis_index("grp")
    share = out.shape[3]
    copy.wait()
    every = filters[...].astype(F32)
    value = every[:, :, :, 0:share]
    for k in range(1, groups):
        value = jnp.where(me == k, every[:, :, :, k * share : (k + 1) * share], value)
    out[...] = value.astype(BF16)


def prepare_kernel(groups, parts, filters, proj, folded, spread, plain):
    def per_step(step, carry):
        taps = [[filters[step, r, c].astype(F32) for c in range(3)] for r in range(3)]
        for p in range(2):
            for near in range(2):
                if p == 0:
                    line = taps[0] if near == 0 else [x + y for x, y in zip(taps[1], taps[2])]
                else:
                    line = [x + y for x, y in zip(taps[0], taps[1])] if near == 0 else taps[2]
                first = jnp.concatenate([line[0] + line[1], line[0]], axis=1)
                second = jnp.concatenate([line[2], line[1] + line[2]], axis=1)
                folded[step, p, near] = jnp.concatenate([first, second], axis=0).astype(BF16)
        return carry

    lax.fori_loop(0, 3, per_step, 0)
    depth, width = proj.shape
    plain[...] = proj[...].astype(F32)
    me, tile = lax.axis_index("grp"), lax.axis_index("tile")
    share = depth // (groups * parts)
    spread[...] = jnp.zeros(spread.shape, BF16)
    for k in range(groups):
        lines = []
        for s in range(parts):
            if parts == 1:
                first = (me ^ k) * share
            else:
                source = tile ^ (s // (parts // 2)) ^ (2 * (s % (parts // 2)))
                first = (source * groups + (me ^ k)) * share
            lines.append(plain[pl.ds(pl.multiple_of(first, 8), share)])
        block = jnp.concatenate(lines, axis=0).astype(BF16)
        height = parts * share
        for phase in range(4):
            spread[
                k, phase * height : (phase + 1) * height, phase * width : (phase + 1) * width
            ] = block


def exchange(values, axis, k):
    size = lax.axis_size(axis)
    return lax.ppermute(values, axis, [(i, i ^ k) for i in range(size)])


def body(latent, coarse_filters, mid_filters, fine_filters, coarse_proj, mid_proj):
    groups, tiles = lax.axis_size("grp"), lax.axis_size("tile")
    me, tile = lax.axis_index("grp"), lax.axis_index("tile")
    frames, rows, cols, depth0 = latent.shape
    depth1, depth2 = mid_proj.shape
    width0 = coarse_filters.shape[4]
    height = groups * rows
    cells = height * frames
    own_mid = mid_filters.shape[4]

    early = []
    divided = own_mid % groups == 0 and (own_mid // groups) % 8 == 0
    share, shares = (own_mid // groups, tiles) if divided else (depth1 // groups, 1)
    lanes = 4 * shares * share
    arrived = [exchange(latent, "grp", k) for k in range(1, groups)]
    arrived = [with_layout_constraint(piece, Layout((0, 1, 2, 3))) for piece in arrived]
    pieces = [jnp.transpose(piece, (1, 2, 0, 3)) for piece in [latent] + arrived]

    mid_rows = jnp.transpose(mid_filters, (0, 1, 2, 4, 3))
    if divided:
        mine = call(
            functools.partial(pick_kernel, groups),
            jax.ShapeDtypeStruct((3, 3, 3, share, depth1), BF16),
            [pltpu.VMEM(mid_rows.shape, BF16), pltpu.SemaphoreType.DMA],
            6 * 10**9,
            10**6,
            mid_rows,
            stay=(0,),
        )
        near = [exchange(mine, "tile", k) for k in range(4, tiles, 2)]
        gathered = jnp.stack([mine, *near])
        early = [exchange(gathered, "tile", 1)]
    else:
        every = lax.all_gather(mid_rows, "tile", axis=3, tiled=True)
        mine = lax.dynamic_slice_in_dim(every, me * share, share, axis=3)[None]

    part = call(
        functools.partial(coarse_kernel, groups),
        jax.ShapeDtypeStruct((cols + 2, cells, width0), BF16),
        [pltpu.VMEM((3, height + 2, cols * frames, depth0), BF16)],
        2 * 10**9,
        10**5,
        *pieces,
        coarse_filters,
    )
    straight = call(
        functools.partial(straight_kernel, groups),
        jax.ShapeDtypeStruct((cols, height, frames, depth1), F32),
        [],
        5 * 10**9,
        10**6,
        *pieces,
        coarse_proj,
    )
    parts = [part] + [exchange(part, "grp", k) for k in range(1, groups)]
    if divided:
        later, _ = lax.optimization_barrier((mine, part))
        beyond = exchange(later, "tile", 2)
    odd_out, even_out, own = call(
        functools.partial(project_kernel, groups),
        (
            jax.ShapeDtypeStruct((2, cells, depth1), BF16),
            jax.ShapeDtypeStruct((2, cells, depth1), BF16),
            jax.ShapeDtypeStruct((cols + 2, cells, depth1), F32),
        ),
        [],
        2 * cells * (cols + 2) * depth0 * depth1,
        2 * 10**6,
        *parts,
        coarse_proj,
        straight,
        *early,
    )
    odd_pairs = [(i, i + 1) for i in range(1, tiles - 1, 2)]
    odd_in = lax.ppermute(odd_out, "tile", odd_pairs + [(j, i) for i, j in odd_pairs])
    even_in = exchange(even_out, "tile", 1)
    if divided:
        gathered, beyond, _ = lax.optimization_barrier((gathered, beyond, own))
        beyond = beyond[None]
        got = early[0]
        mine = jnp.concatenate(
            [gathered[:1], beyond, gathered[1:], got[:1], exchange(beyond, "tile", 1), got[1:]]
        )
    mid_folded = call(
        fold_middle_kernel,
        jax.ShapeDtypeStruct((3, 3, 2, depth1, lanes), BF16),
        [],
        10**6,
        4 * 10**6,
        mine,
    )
    local = (rows + 2) * frames
    *chunks, block = call(
        functools.partial(middle_kernel, groups, rows, frames),
        tuple(
            jax.ShapeDtypeStruct(((cols + 1) * (rows + 1) * frames, lanes), BF16)
            for _ in range(groups)
        )
        + (jax.ShapeDtypeStruct((cols + 2, local, depth1), BF16),),
        [
            pltpu.VMEM((3, cols + 2, cells + 2 * frames, depth1), BF16),
            pltpu.VMEM((3, cols + 2, cells, depth1), BF16),
            pltpu.VMEM((cols + 2, height + 2, frames, depth1), F32),
            pltpu.VMEM((cols + 1, height + 2, frames, lanes), F32),
        ],
        2 * 18 * (cols + 1) * cells * depth1 * lanes,
        5 * 10**6,
        odd_in,
        even_in,
        own,
        mid_folded,
    )
    chunks = [chunks[0]] + [exchange(chunks[k], "grp", k) for k in range(1, groups)]
    fine_folded, spread = call(
        functools.partial(prepare_kernel, groups, shares),
        (
            jax.ShapeDtypeStruct((3, 2, 2, 2 * depth2, 2 * depth2), BF16),
            jax.ShapeDtypeStruct((groups, lanes, 4 * depth2), BF16),
        ),
        [pltpu.VMEM((depth1, depth2), F32)],
        10**6,
        4 * 10**6,
        fine_filters,
        mid_proj,
    )
    tall, broad = 2 * rows, 2 * cols
    return call(
        functools.partial(fine_kernel, groups, frames),
        jax.ShapeDtypeStruct((frames, 2 * tall, 2 * broad, depth2), BF16),
        [
            pltpu.VMEM((3, broad + 2, (tall + 2) * frames, depth2), BF16),
            pltpu.VMEM((3, broad + 2, tall * frames, depth2), BF16),
            pltpu.VMEM((broad + 2, tall, frames, depth2), F32),
        ],
        2 * 24 * (broad + 1) * tall * frames * depth2 * 2 * depth2,
        3 * 10**6,
        *[chunks[k] for k in chunk_order(groups)],
        block,
        spread,
        mid_proj,
        fine_folded,
    )


def solution(mesh):
    in_specs = (
        P(None, "grp", "tile", None),
        P(None, None, None, None, "grp"),
        P(None, None, None, None, "tile"),
        P(),
        P(),
        P(),
    )
    out_specs = P(None, "grp", "tile", None)
    return jax.shard_map(body, mesh=mesh, in_specs=in_specs, out_specs=out_specs, check_vma=False)
```

```python
import functools

import jax
import jax.numpy as jnp
from jax import lax
from jax.experimental import pallas as pl
from jax.experimental.layout import Layout, with_layout_constraint
from jax.experimental.pallas import tpu as pltpu
from jax.sharding import PartitionSpec as P

VMEM = pl.BlockSpec(memory_space=pltpu.VMEM)
FAR = pl.BlockSpec(memory_space=pltpu.HBM)
F32 = jnp.float32
BF16 = jnp.bfloat16


def call(kernel, outs, scratch, flops, nbytes, *args, stay=(), far_out=False):
    args = [
        pltpu.with_memory_space_constraint(arg, pltpu.HBM) if n in stay else arg
        for n, arg in enumerate(args)
    ]
    return pl.pallas_call(
        kernel,
        out_shape=outs,
        in_specs=[FAR if n in stay else VMEM for n in range(len(args))],
        out_specs=jax.tree.map(lambda _: FAR if far_out else VMEM, outs),
        scratch_shapes=scratch,
        compiler_params=pltpu.CompilerParams(vmem_limit_bytes=40 << 20),
        cost_estimate=pl.CostEstimate(flops=flops, bytes_accessed=nbytes, transcendentals=0),
    )(*args)


def dot(left, right):
    return jnp.dot(left, right, preferred_element_type=F32)


def activate(values):
    scaled = values * lax.rsqrt(jnp.mean(values * values, axis=-1, keepdims=True) + 1e-06)
    return scaled / (1.0 + jnp.exp(-scaled))


def delayed(values, steps):
    if steps == 0:
        return values
    axis = values.ndim - 2
    frame = lax.broadcasted_iota(jnp.int32, values.shape, axis)
    return jnp.where(frame >= steps, pltpu.roll(values, steps, axis), 0.0)


def coarse_kernel(groups, *refs):
    pieces, (filters, part, shifted) = refs[:groups], refs[groups:]
    rows, cols, frames, depth = pieces[0].shape
    width = filters.shape[4]
    height = groups * rows
    me = lax.axis_index("grp")
    edge = jnp.zeros((1, cols * frames, depth), BF16)
    for step in range(3):
        shifted[step, 0:1] = edge
        shifted[step, height + 1 : height + 2] = edge
    for k in range(groups):
        at = (me ^ k) * rows
        raw = pieces[k][...]
        act = activate(raw.astype(F32))
        for step in range(3):
            moved = delayed(act, 2 - step).reshape(rows, cols * frames, depth)
            shifted[step, pl.ds(at + 1, rows)] = moved.astype(BF16)
    if width % 128 == 0:
        total = None
        for step in range(3):
            left = shifted[step, 1 : height + 1].reshape(height * cols * frames, depth)
            taps = [filters[step, row, col] for row in range(3) for col in range(3)]
            term = dot(left, jnp.concatenate(taps, axis=1))
            total = term if total is None else total + term
        total = total.reshape(height, cols * frames, 9 * width)
        above, level, below = [total[:, :, 3 * n * width : 3 * (n + 1) * width] for n in range(3)]
        nothing = jnp.zeros((1, cols * frames, 3 * width), F32)
        total = (
            level
            + jnp.concatenate([nothing, above[:-1]], axis=0)
            + jnp.concatenate([below[1:], nothing], axis=0)
        )
        totals = [total[:, :, n * width : (n + 1) * width] for n in range(3)]
    else:
        totals = [None] * 3
        for step in range(3):
            for row in range(3):
                left = shifted[step, row : row + height].reshape(height * cols * frames, depth)
                for col in range(3):
                    term = dot(left, filters[step, row, col])
                    totals[col] = term if totals[col] is None else totals[col] + term
    totals = [total.reshape(height, cols, frames, width) for total in totals]
    for out in range(cols + 2):
        value = sum(
            totals[tap][:, out - 2 + tap] for tap in range(3) if 0 <= out - 2 + tap < cols
        )
        part[out] = value.reshape(height * frames, width).astype(BF16)


def straight_kernel(groups, *refs):
    pieces, (proj, straight) = refs[:groups], refs[groups:]
    rows, cols, frames, depth = pieces[0].shape
    me = lax.axis_index("grp")
    for k in range(groups):
        flat = pieces[k][...].reshape(rows * cols * frames, depth)
        direct = dot(flat, proj[...]).reshape(rows, cols, frames, proj.shape[1])
        for col in range(cols):
            straight[col, pl.ds((me ^ k) * rows, rows)] = direct[:, col]


def project_kernel(groups, *refs):
    parts, (proj, straight), (odd_out, even_out, own) = (
        refs[:groups], refs[groups : groups + 2], refs[-3:],
    )
    extent, cells, width = parts[0].shape
    outputs = proj.shape[1]
    me = lax.axis_index("grp")
    total = None
    for k in range(groups):
        weights = proj[pl.ds(pl.multiple_of((me ^ k) * width, width), width)]
        term = dot(parts[k][...].reshape(extent * cells, width), weights)
        total = term if total is None else total + term
    total = total.reshape(extent, cells, outputs)
    cols = extent - 2
    middle = total[1 : cols + 1] + straight[...].reshape(cols, cells, outputs)
    own[0] = total[0]
    own[1 : cols + 1] = middle
    own[cols + 1] = total[cols + 1]
    left = jnp.stack([total[0], middle[0]])
    right = jnp.stack([middle[cols - 1], total[cols + 1]])
    odd = lax.axis_index("tile") % 2 == 1
    even_out[...] = jnp.where(odd, left, right).astype(BF16)
    odd_out[...] = jnp.where(odd, right, left).astype(BF16)


def middle_kernel(groups, rows, frames, odd_in, even_in, own, filters, *refs):
    outs, (block, acts, acts_odd, kept, sums) = refs[:groups], refs[groups:]
    extent, cells, depth = own.shape
    cols = extent - 2
    height = cells // frames
    me = lax.axis_index("grp")
    tile = lax.axis_index("tile")
    odd = tile % 2 == 1
    even_got = even_in[...].astype(F32)
    odd_got = odd_in[...].astype(F32)
    from_left = jnp.where(odd, even_got, odd_got)
    from_right = jnp.where(odd, odd_got, even_got)
    values = []
    for col in range(extent):
        value = own[col]
        if col < 2:
            value = value + from_left[col]
        if col >= cols:
            value = value + from_right[col - cols]
        if col == 0:
            value = jnp.where(tile == 0, 0.0, value)
        if col == extent - 1:
            value = jnp.where(tile == lax.axis_size("tile") - 1, 0.0, value)
        values.append(value.astype(BF16).astype(F32).reshape(height, frames, depth))
    nothing = jnp.zeros((1, frames, depth), F32)
    for col in range(extent):
        kept[col, 0:1] = nothing
        kept[col, 1 : height + 1] = values[col]
        kept[col, height + 1 : height + 2] = nothing
        act = activate(values[col])
        for step in range(3):
            moved = delayed(act, 2 - step)
            framed = jnp.concatenate([nothing, moved, nothing], axis=0)
            acts[step, col] = framed.reshape(cells + 2 * frames, depth).astype(BF16)
            acts_odd[step, col] = moved.reshape(cells, depth).astype(BF16)
    block[...] = (
        kept[:, pl.ds(me * rows, rows + 2)]
        .reshape(extent, (rows + 2) * frames, depth)
        .astype(BF16)
    )
    pairs = extent - 1
    total = None
    for step in range(3):
        for row in range(3):
            for side in range(2):
                if row == 1:
                    left = acts_odd[step, side : side + pairs]
                else:
                    first = row * frames
                    left = acts[step, side : side + pairs, first : first + cells]
                term = dot(left.reshape(pairs * cells, depth), filters[step, row, side])
                total = term if total is None else total + term
    lanes = total.shape[1]
    total = total.reshape(pairs, height, frames, lanes)
    empty = jnp.zeros((pairs, 1, frames, lanes), F32)
    sums[:, 0:1] = empty
    sums[:, 1 : height + 1] = total
    sums[:, height + 1 : height + 2] = empty
    half = lanes // 2
    for k in range(groups):
        chunk = sums[:, pl.ds((me ^ k) * rows, rows + 2)]
        ends = jnp.concatenate([chunk[:, rows + 1 :, :, :half], chunk[:, :1, :, half:]], axis=3)
        chunk = jnp.concatenate([ends, chunk[:, 1 : rows + 1]], axis=1)
        outs[k][...] = chunk.reshape(pairs * (rows + 1) * frames, lanes).astype(BF16)


def chunk_order(groups):
    return [0, *range(2, groups), 1]


def fine_kernel(groups, frames, *refs):
    chunks = dict(zip(chunk_order(groups), refs[:groups]))
    base, spread, filters, out, acts, acts_odd, lows, ready, sent = refs[groups:]
    extent, rows = base.shape[0], base.shape[1] - 2
    pairs = extent - 1
    width = base.shape[3]
    tall, broad = 2 * rows, 2 * (extent - 2)
    me, last_me = lax.axis_index("grp"), lax.axis_size("grp") - 1
    tile, last_tile = lax.axis_index("tile"), lax.axis_size("tile") - 1
    total = None
    for k in range(groups):
        term = dot(chunks[k][...], spread[k])
        total = term if total is None else total + term
    total = total.reshape(pairs, rows + 1, frames, 4 * width)
    nothing = jnp.zeros((1, frames, width), F32)
    for col in range(broad + 2):
        pair, side = divmod(col, 2)
        upper, lower = [
            total[pair, :, :, (2 * p + side) * width : (2 * p + side + 1) * width]
            for p in range(2)
        ]
        lower = lower + base[pair + side, : rows + 1]
        upper = jnp.concatenate([upper[1:], upper[:1]], axis=0) + base[pair + side, 1:]
        woven = jnp.stack([lower, upper], axis=1)
        value = woven.reshape(tall + 2, frames, width).astype(BF16).astype(F32)
        if col == 0:
            value = jnp.where(tile == 0, 0.0, value)
        if col == broad + 1:
            value = jnp.where(tile == last_tile, 0.0, value)
        top = jnp.where(me == 0, 0.0, value[0:1])
        bottom = jnp.where(me == last_me, 0.0, value[tall + 1 : tall + 2])
        value = jnp.concatenate([top, value[1 : tall + 1], bottom], axis=0)
        lows[col] = value[1 : tall + 1]
        act = activate(value)
        for step in range(3):
            moved = delayed(act, 2 - step)
            acts[step, col] = moved.reshape((tall + 2) * frames, width).astype(BF16)
            acts_odd[step, col] = (
                moved[1 : tall + 1].reshape(tall * frames, width).astype(BF16)
            )
    span = broad + 1
    strip = tall * frames
    for p in range(2):
        sums = None
        for step in range(3):
            for near in range(2):
                row = p + near
                if row == 1:
                    pick = [acts_odd[step, side : side + span] for side in range(2)]
                else:
                    first = row * frames
                    pick = [
                        acts[step, side : side + span, first : first + strip]
                        for side in range(2)
                    ]
                left = jnp.concatenate([v.reshape(span * strip, width) for v in pick], axis=1)
                term = dot(left, filters[step, p, near])
                sums = term if sums is None else sums + term
        sums = sums.reshape(span, tall, frames, 2 * width)
        fields = []
        for col in range(2 * broad):
            pair, side = divmod(col + 1, 2)
            low = lows[pair + side]
            fields.append(sums[pair, :, :, side * width : (side + 1) * width] + low)
        field = jnp.stack(fields, axis=1)
        for row in range(tall):
            ready[p, :, row] = jnp.swapaxes(field[row], 0, 1).astype(BF16)
        pltpu.make_async_copy(ready.at[p], out.at[:, :, p], sent.at[p]).start()
    for p in range(2):
        pltpu.make_async_copy(ready.at[p], out.at[:, :, p], sent.at[p]).wait()


def fold_middle_kernel(pieces, out):
    parts, n, depth = pieces.shape[0], pieces.shape[4], pieces.shape[5]

    def per_step(step, carry):
        taps = [
            [
                pieces[:, step, row, col].astype(F32).reshape(parts * n, depth)
                for col in range(3)
            ]
            for row in range(3)
        ]
        nothing = jnp.zeros((parts * n, depth), F32)
        for side in range(2):
            narrow = [
                [taps[r][0] + taps[r][1] if side == 0 else taps[r][2],
                 taps[r][0] if side == 0 else taps[r][1] + taps[r][2]]
                for r in range(3)
            ]
            for row in range(3):
                blocks = []
                for p in range(2):
                    for q in range(2):
                        if row == 1:
                            value = narrow[1][q] + narrow[2 if p == 0 else 0][q]
                        elif row == 0:
                            value = narrow[0][q] if p == 0 else nothing
                        else:
                            value = nothing if p == 0 else narrow[2][q]
                        blocks.append(value)
                out[step, row, side] = jnp.concatenate(blocks, axis=0).T.astype(BF16)
        return carry

    lax.fori_loop(0, 3, per_step, 0)


def pick_kernel(groups, stored, out, filters, arrived):
    copy = pltpu.make_async_copy(stored, filters, arrived)
    copy.start()
    me = lax.axis_index("grp")
    share = out.shape[3]
    copy.wait()
    every = filters[...].astype(F32)
    value = every[:, :, :, 0:share]
    for k in range(1, groups):
        value = jnp.where(me == k, every[:, :, :, k * share : (k + 1) * share], value)
    out[...] = value.astype(BF16)


def prepare_kernel(groups, parts, frames, block, filters, proj, folded, spread, base, plain):
    extent, cells, wide = block.shape
    low = dot(block[...].reshape(extent * cells, wide), proj[...])
    base[...] = low.reshape(base.shape)
    def per_step(step, carry):
        taps = [[filters[step, r, c].astype(F32) for c in range(3)] for r in range(3)]
        for p in range(2):
            for near in range(2):
                if p == 0:
                    line = taps[0] if near == 0 else [x + y for x, y in zip(taps[1], taps[2])]
                else:
                    line = [x + y for x, y in zip(taps[0], taps[1])] if near == 0 else taps[2]
                first = jnp.concatenate([line[0] + line[1], line[0]], axis=1)
                second = jnp.concatenate([line[2], line[1] + line[2]], axis=1)
                folded[step, p, near] = jnp.concatenate([first, second], axis=0).astype(BF16)
        return carry

    lax.fori_loop(0, 3, per_step, 0)
    depth, width = proj.shape
    plain[...] = proj[...].astype(F32)
    me, tile = lax.axis_index("grp"), lax.axis_index("tile")
    share = depth // (groups * parts)
    spread[...] = jnp.zeros(spread.shape, BF16)
    for k in range(groups):
        lines = []
        for s in range(parts):
            if parts == 1:
                first = (me ^ k) * share
            else:
                source = tile ^ (s // (parts // 2)) ^ (2 * (s % (parts // 2)))
                first = (source * groups + (me ^ k)) * share
            lines.append(plain[pl.ds(pl.multiple_of(first, 8), share)])
        block = jnp.concatenate(lines, axis=0).astype(BF16)
        height = parts * share
        for phase in range(4):
            spread[
                k, phase * height : (phase + 1) * height, phase * width : (phase + 1) * width
            ] = block


def exchange(values, axis, k):
    size = lax.axis_size(axis)
    return lax.ppermute(values, axis, [(i, i ^ k) for i in range(size)])


def body(latent, coarse_filters, mid_filters, fine_filters, coarse_proj, mid_proj):
    groups, tiles = lax.axis_size("grp"), lax.axis_size("tile")
    me, tile = lax.axis_index("grp"), lax.axis_index("tile")
    frames, rows, cols, depth0 = latent.shape
    depth1, depth2 = mid_proj.shape
    width0 = coarse_filters.shape[4]
    height = groups * rows
    cells = height * frames
    own_mid = mid_filters.shape[4]

    early = []
    divided = own_mid % groups == 0 and (own_mid // groups) % 8 == 0
    share, shares = (own_mid // groups, tiles) if divided else (depth1 // groups, 1)
    lanes = 4 * shares * share
    arrived = [exchange(latent, "grp", k) for k in range(1, groups)]
    arrived = [with_layout_constraint(piece, Layout((0, 1, 2, 3))) for piece in arrived]
    pieces = [jnp.transpose(piece, (1, 2, 0, 3)) for piece in [latent] + arrived]

    mid_rows = jnp.transpose(mid_filters, (0, 1, 2, 4, 3))
    if divided:
        mine = call(
            functools.partial(pick_kernel, groups),
            jax.ShapeDtypeStruct((3, 3, 3, share, depth1), BF16),
            [pltpu.VMEM(mid_rows.shape, BF16), pltpu.SemaphoreType.DMA],
            6 * 10**9,
            10**6,
            mid_rows,
            stay=(0,),
        )
        near = [exchange(mine, "tile", k) for k in range(4, tiles, 2)]
        gathered = jnp.stack([mine, *near])
        early = [exchange(gathered, "tile", 1)]
    else:
        every = lax.all_gather(mid_rows, "tile", axis=3, tiled=True)
        mine = lax.dynamic_slice_in_dim(every, me * share, share, axis=3)[None]

    part = call(
        functools.partial(coarse_kernel, groups),
        jax.ShapeDtypeStruct((cols + 2, cells, width0), BF16),
        [pltpu.VMEM((3, height + 2, cols * frames, depth0), BF16)],
        2 * 10**9,
        10**5,
        *pieces,
        coarse_filters,
    )
    straight = call(
        functools.partial(straight_kernel, groups),
        jax.ShapeDtypeStruct((cols, height, frames, depth1), F32),
        [],
        5 * 10**9,
        10**6,
        *pieces,
        coarse_proj,
    )
    parts = [part] + [exchange(part, "grp", k) for k in range(1, groups)]
    if divided:
        later, _ = lax.optimization_barrier((mine, part))
        beyond = exchange(later, "tile", 2)
    odd_out, even_out, own = call(
        functools.partial(project_kernel, groups),
        (
            jax.ShapeDtypeStruct((2, cells, depth1), BF16),
            jax.ShapeDtypeStruct((2, cells, depth1), BF16),
            jax.ShapeDtypeStruct((cols + 2, cells, depth1), F32),
        ),
        [],
        2 * cells * (cols + 2) * depth0 * depth1,
        2 * 10**6,
        *parts,
        coarse_proj,
        straight,
        *early,
    )
    odd_pairs = [(i, i + 1) for i in range(1, tiles - 1, 2)]
    odd_in = lax.ppermute(odd_out, "tile", odd_pairs + [(j, i) for i, j in odd_pairs])
    even_in = exchange(even_out, "tile", 1)
    if divided:
        gathered, beyond, _ = lax.optimization_barrier((gathered, beyond, own))
        beyond = beyond[None]
        got = early[0]
        mine = jnp.concatenate(
            [gathered[:1], beyond, gathered[1:], got[:1], exchange(beyond, "tile", 1), got[1:]]
        )
    mid_folded = call(
        fold_middle_kernel,
        jax.ShapeDtypeStruct((3, 3, 2, depth1, lanes), BF16),
        [],
        10**6,
        4 * 10**6,
        mine,
    )
    local = (rows + 2) * frames
    *chunks, block = call(
        functools.partial(middle_kernel, groups, rows, frames),
        tuple(
            jax.ShapeDtypeStruct(((cols + 1) * (rows + 1) * frames, lanes), BF16)
            for _ in range(groups)
        )
        + (jax.ShapeDtypeStruct((cols + 2, local, depth1), BF16),),
        [
            pltpu.VMEM((3, cols + 2, cells + 2 * frames, depth1), BF16),
            pltpu.VMEM((3, cols + 2, cells, depth1), BF16),
            pltpu.VMEM((cols + 2, height + 2, frames, depth1), F32),
            pltpu.VMEM((cols + 1, height + 2, frames, lanes), F32),
        ],
        2 * 18 * (cols + 1) * cells * depth1 * lanes,
        5 * 10**6,
        odd_in,
        even_in,
        own,
        mid_folded,
    )
    chunks = [chunks[0]] + [exchange(chunks[k], "grp", k) for k in range(1, groups)]
    fine_folded, spread, base = call(
        functools.partial(prepare_kernel, groups, shares, frames),
        (
            jax.ShapeDtypeStruct((3, 2, 2, 2 * depth2, 2 * depth2), BF16),
            jax.ShapeDtypeStruct((groups, lanes, 4 * depth2), BF16),
            jax.ShapeDtypeStruct((cols + 2, rows + 2, frames, depth2), F32),
        ),
        [pltpu.VMEM((depth1, depth2), F32)],
        10**6,
        4 * 10**6,
        block,
        fine_filters,
        mid_proj,
    )
    tall, broad = 2 * rows, 2 * cols
    out = call(
        functools.partial(fine_kernel, groups, frames),
        jax.ShapeDtypeStruct((frames, tall, 2, 2 * broad, depth2), BF16),
        [
            pltpu.VMEM((3, broad + 2, (tall + 2) * frames, depth2), BF16),
            pltpu.VMEM((3, broad + 2, tall * frames, depth2), BF16),
            pltpu.VMEM((broad + 2, tall, frames, depth2), F32),
            pltpu.VMEM((2, frames, tall, 2 * broad, depth2), BF16),
            pltpu.SemaphoreType.DMA((2,)),
        ],
        2 * 24 * (broad + 1) * tall * frames * depth2 * 2 * depth2,
        3 * 10**6,
        *[chunks[k] for k in chunk_order(groups)],
        base,
        spread,
        fine_folded,
        far_out=True,
    )
    return out.reshape(frames, 2 * tall, 2 * broad, depth2)


def solution(mesh):
    in_specs = (
        P(None, "grp", "tile", None),
        P(None, None, None, None, "grp"),
        P(None, None, None, None, "tile"),
        P(),
        P(),
        P(),
    )
    out_specs = P(None, "grp", "tile", None)
    return jax.shard_map(body, mesh=mesh, in_specs=in_specs, out_specs=out_specs, check_vma=False)
```

```python
import functools

import jax
import jax.numpy as jnp
from jax import lax
from jax.experimental import pallas as pl
from jax.experimental.layout import Layout, with_layout_constraint
from jax.experimental.pallas import tpu as pltpu
from jax.sharding import PartitionSpec as P

VMEM = pl.BlockSpec(memory_space=pltpu.VMEM)
FAR = pl.BlockSpec(memory_space=pltpu.HBM)
F32 = jnp.float32
BF16 = jnp.bfloat16


def call(kernel, outs, scratch, flops, nbytes, *args, stay=()):
    args = [
        pltpu.with_memory_space_constraint(arg, pltpu.HBM) if n in stay else arg
        for n, arg in enumerate(args)
    ]
    return pl.pallas_call(
        kernel,
        out_shape=outs,
        in_specs=[FAR if n in stay else VMEM for n in range(len(args))],
        out_specs=jax.tree.map(lambda _: VMEM, outs),
        scratch_shapes=scratch,
        compiler_params=pltpu.CompilerParams(vmem_limit_bytes=40 << 20),
        cost_estimate=pl.CostEstimate(flops=flops, bytes_accessed=nbytes, transcendentals=0),
    )(*args)


def dot(left, right):
    return jnp.dot(left, right, preferred_element_type=F32)


def activate(values):
    scaled = values * lax.rsqrt(jnp.mean(values * values, axis=-1, keepdims=True) + 1e-06)
    return scaled / (1.0 + jnp.exp(-scaled))


def delayed(values, steps):
    if steps == 0:
        return values
    axis = values.ndim - 2
    frame = lax.broadcasted_iota(jnp.int32, values.shape, axis)
    return jnp.where(frame >= steps, pltpu.roll(values, steps, axis), 0.0)


def coarse_kernel(groups, *refs):
    pieces, (filters, part, shifted) = refs[:groups], refs[groups:]
    rows, cols, frames, depth = pieces[0].shape
    width = filters.shape[4]
    height = groups * rows
    me = lax.axis_index("grp")
    edge = jnp.zeros((1, cols * frames, depth), BF16)
    for step in range(3):
        shifted[step, 0:1] = edge
        shifted[step, height + 1 : height + 2] = edge
    for k in range(groups):
        at = (me ^ k) * rows
        raw = pieces[k][...]
        act = activate(raw.astype(F32))
        for step in range(3):
            moved = delayed(act, 2 - step).reshape(rows, cols * frames, depth)
            shifted[step, pl.ds(at + 1, rows)] = moved.astype(BF16)
    if width % 128 == 0:
        total = None
        for step in range(3):
            left = shifted[step, 1 : height + 1].reshape(height * cols * frames, depth)
            taps = [filters[step, row, col] for row in range(3) for col in range(3)]
            term = dot(left, jnp.concatenate(taps, axis=1))
            total = term if total is None else total + term
        total = total.reshape(height, cols * frames, 9 * width)
        above, level, below = [total[:, :, 3 * n * width : 3 * (n + 1) * width] for n in range(3)]
        nothing = jnp.zeros((1, cols * frames, 3 * width), F32)
        total = (
            level
            + jnp.concatenate([nothing, above[:-1]], axis=0)
            + jnp.concatenate([below[1:], nothing], axis=0)
        )
        totals = [total[:, :, n * width : (n + 1) * width] for n in range(3)]
    else:
        totals = [None] * 3
        for step in range(3):
            for row in range(3):
                left = shifted[step, row : row + height].reshape(height * cols * frames, depth)
                for col in range(3):
                    term = dot(left, filters[step, row, col])
                    totals[col] = term if totals[col] is None else totals[col] + term
    totals = [total.reshape(height, cols, frames, width) for total in totals]
    for out in range(cols + 2):
        value = sum(
            totals[tap][:, out - 2 + tap] for tap in range(3) if 0 <= out - 2 + tap < cols
        )
        part[out] = value.reshape(height * frames, width).astype(BF16)


def straight_kernel(groups, *refs):
    pieces, (proj, straight) = refs[:groups], refs[groups:]
    rows, cols, frames, depth = pieces[0].shape
    me = lax.axis_index("grp")
    for k in range(groups):
        flat = pieces[k][...].reshape(rows * cols * frames, depth)
        direct = dot(flat, proj[...]).reshape(rows, cols, frames, proj.shape[1])
        for col in range(cols):
            straight[col, pl.ds((me ^ k) * rows, rows)] = direct[:, col]


def project_kernel(groups, *refs):
    parts, (proj, straight), (odd_out, even_out, own) = (
        refs[:groups], refs[groups : groups + 2], refs[-3:],
    )
    extent, cells, width = parts[0].shape
    outputs = proj.shape[1]
    me = lax.axis_index("grp")
    total = None
    for k in range(groups):
        weights = proj[pl.ds(pl.multiple_of((me ^ k) * width, width), width)]
        term = dot(parts[k][...].reshape(extent * cells, width), weights)
        total = term if total is None else total + term
    total = total.reshape(extent, cells, outputs)
    cols = extent - 2
    middle = total[1 : cols + 1] + straight[...].reshape(cols, cells, outputs)
    own[0] = total[0].astype(BF16)
    own[1 : cols + 1] = middle.astype(BF16)
    own[cols + 1] = total[cols + 1].astype(BF16)
    left = jnp.stack([total[0], middle[0]])
    right = jnp.stack([middle[cols - 1], total[cols + 1]])
    odd = lax.axis_index("tile") % 2 == 1
    even_out[...] = jnp.where(odd, left, right).astype(BF16)
    odd_out[...] = jnp.where(odd, right, left).astype(BF16)


def middle_kernel(groups, rows, frames, odd_in, even_in, own, filters, *refs):
    outs, (block, acts, acts_odd, kept, sums) = refs[:groups], refs[groups:]
    extent, cells, depth = own.shape
    cols = extent - 2
    height = cells // frames
    me = lax.axis_index("grp")
    tile = lax.axis_index("tile")
    odd = tile % 2 == 1
    even_got = even_in[...].astype(F32)
    odd_got = odd_in[...].astype(F32)
    from_left = jnp.where(odd, even_got, odd_got)
    from_right = jnp.where(odd, odd_got, even_got)
    values = []
    for col in range(extent):
        value = own[col].astype(F32)
        if col < 2:
            value = value + from_left[col]
        if col >= cols:
            value = value + from_right[col - cols]
        if col == 0:
            value = jnp.where(tile == 0, 0.0, value)
        if col == extent - 1:
            value = jnp.where(tile == lax.axis_size("tile") - 1, 0.0, value)
        values.append(value.astype(BF16).astype(F32).reshape(height, frames, depth))
    nothing = jnp.zeros((1, frames, depth), F32)
    for col in range(extent):
        kept[col, 0:1] = nothing
        kept[col, 1 : height + 1] = values[col]
        kept[col, height + 1 : height + 2] = nothing
        act = activate(values[col])
        for step in range(3):
            moved = delayed(act, 2 - step)
            framed = jnp.concatenate([nothing, moved, nothing], axis=0)
            acts[step, col] = framed.reshape(cells + 2 * frames, depth).astype(BF16)
            acts_odd[step, col] = moved.reshape(cells, depth).astype(BF16)
    block[...] = (
        kept[:, pl.ds(me * rows, rows + 2)]
        .reshape(extent, (rows + 2) * frames, depth)
        .astype(BF16)
    )
    pairs = extent - 1
    total = None
    for step in range(3):
        for row in range(3):
            for side in range(2):
                if row == 1:
                    left = acts_odd[step, side : side + pairs]
                else:
                    first = row * frames
                    left = acts[step, side : side + pairs, first : first + cells]
                term = dot(left.reshape(pairs * cells, depth), filters[step, row, side])
                total = term if total is None else total + term
    lanes = total.shape[1]
    total = total.reshape(pairs, height, frames, lanes)
    empty = jnp.zeros((pairs, 1, frames, lanes), F32)
    sums[:, 0:1] = empty
    sums[:, 1 : height + 1] = total
    sums[:, height + 1 : height + 2] = empty
    half = lanes // 2
    for k in range(groups):
        chunk = sums[:, pl.ds((me ^ k) * rows, rows + 2)]
        ends = jnp.concatenate([chunk[:, rows + 1 :, :, :half], chunk[:, :1, :, half:]], axis=3)
        chunk = jnp.concatenate([ends, chunk[:, 1 : rows + 1]], axis=1)
        outs[k][...] = chunk.reshape(pairs * (rows + 1) * frames, lanes).astype(BF16)


def chunk_order(groups):
    return [0, *range(2, groups), 1]


def fine_kernel(groups, frames, *refs):
    chunks = dict(zip(chunk_order(groups), refs[:groups]))
    block, spread, proj, filters, out, acts, acts_odd, lows = refs[groups:]
    extent, cells = block.shape[:2]
    pairs, rows = extent - 1, cells // frames - 2
    width = proj.shape[1]
    tall, broad = 2 * rows, 2 * (extent - 2)
    me, last_me = lax.axis_index("grp"), lax.axis_size("grp") - 1
    tile, last_tile = lax.axis_index("tile"), lax.axis_size("tile") - 1
    total = None
    for k in range(groups):
        term = dot(chunks[k][...], spread[k])
        total = term if total is None else total + term
    total = total.reshape(pairs, rows + 1, frames, 4 * width)
    base = dot(block[...].reshape(extent * cells, block.shape[2]), proj[...])
    base = base.reshape(extent, rows + 2, frames, width)
    nothing = jnp.zeros((1, frames, width), F32)
    for col in range(broad + 2):
        pair, side = divmod(col, 2)
        upper, lower = [
            total[pair, :, :, (2 * p + side) * width : (2 * p + side + 1) * width]
            for p in range(2)
        ]
        lower = lower + base[pair + side, : rows + 1]
        upper = jnp.concatenate([upper[1:], upper[:1]], axis=0) + base[pair + side, 1:]
        woven = jnp.stack([lower, upper], axis=1)
        value = woven.reshape(tall + 2, frames, width).astype(BF16).astype(F32)
        if col == 0:
            value = jnp.where(tile == 0, 0.0, value)
        if col == broad + 1:
            value = jnp.where(tile == last_tile, 0.0, value)
        top = jnp.where(me == 0, 0.0, value[0:1])
        bottom = jnp.where(me == last_me, 0.0, value[tall + 1 : tall + 2])
        value = jnp.concatenate([top, value[1 : tall + 1], bottom], axis=0)
        lows[col] = value[1 : tall + 1]
        act = activate(value)
        for step in range(3):
            moved = delayed(act, 2 - step)
            acts[step, col] = moved.reshape((tall + 2) * frames, width).astype(BF16)
            acts_odd[step, col] = (
                moved[1 : tall + 1].reshape(tall * frames, width).astype(BF16)
            )
    span = broad + 1
    strip = tall * frames
    for p in range(2):
        sums = None
        for step in range(3):
            for near in range(2):
                row = p + near
                if row == 1:
                    pick = [acts_odd[step, side : side + span] for side in range(2)]
                else:
                    first = row * frames
                    pick = [
                        acts[step, side : side + span, first : first + strip]
                        for side in range(2)
                    ]
                left = jnp.concatenate([v.reshape(span * strip, width) for v in pick], axis=1)
                term = dot(left, filters[step, p, near])
                sums = term if sums is None else sums + term
        sums = sums.reshape(span, tall, frames, 2 * width)
        fields = []
        for col in range(2 * broad):
            pair, side = divmod(col + 1, 2)
            low = lows[pair + side]
            fields.append(sums[pair, :, :, side * width : (side + 1) * width] + low)
        field = jnp.stack(fields, axis=1)
        for row in range(tall):
            out[:, 2 * row + p] = jnp.swapaxes(field[row], 0, 1).astype(BF16)


def fold_middle_kernel(pieces, out):
    parts, n, depth = pieces.shape[0], pieces.shape[4], pieces.shape[5]

    def per_step(step, carry):
        taps = [
            [
                pieces[:, step, row, col].astype(F32).reshape(parts * n, depth)
                for col in range(3)
            ]
            for row in range(3)
        ]
        nothing = jnp.zeros((parts * n, depth), F32)
        for side in range(2):
            narrow = [
                [taps[r][0] + taps[r][1] if side == 0 else taps[r][2],
                 taps[r][0] if side == 0 else taps[r][1] + taps[r][2]]
                for r in range(3)
            ]
            for row in range(3):
                blocks = []
                for p in range(2):
                    for q in range(2):
                        if row == 1:
                            value = narrow[1][q] + narrow[2 if p == 0 else 0][q]
                        elif row == 0:
                            value = narrow[0][q] if p == 0 else nothing
                        else:
                            value = nothing if p == 0 else narrow[2][q]
                        blocks.append(value)
                out[step, row, side] = jnp.concatenate(blocks, axis=0).T.astype(BF16)
        return carry

    lax.fori_loop(0, 3, per_step, 0)


def pick_kernel(groups, stored, out, filters, arrived):
    copy = pltpu.make_async_copy(stored, filters, arrived)
    copy.start()
    me = lax.axis_index("grp")
    share = out.shape[3]
    copy.wait()
    every = filters[...].astype(F32)
    value = every[:, :, :, 0:share]
    for k in range(1, groups):
        value = jnp.where(me == k, every[:, :, :, k * share : (k + 1) * share], value)
    out[...] = value.astype(BF16)


def prepare_kernel(groups, parts, filters, proj, folded, spread, plain):
    def per_step(step, carry):
        taps = [[filters[step, r, c].astype(F32) for c in range(3)] for r in range(3)]
        for p in range(2):
            for near in range(2):
                if p == 0:
                    line = taps[0] if near == 0 else [x + y for x, y in zip(taps[1], taps[2])]
                else:
                    line = [x + y for x, y in zip(taps[0], taps[1])] if near == 0 else taps[2]
                first = jnp.concatenate([line[0] + line[1], line[0]], axis=1)
                second = jnp.concatenate([line[2], line[1] + line[2]], axis=1)
                folded[step, p, near] = jnp.concatenate([first, second], axis=0).astype(BF16)
        return carry

    lax.fori_loop(0, 3, per_step, 0)
    depth, width = proj.shape
    plain[...] = proj[...].astype(F32)
    me, tile = lax.axis_index("grp"), lax.axis_index("tile")
    share = depth // (groups * parts)
    spread[...] = jnp.zeros(spread.shape, BF16)
    for k in range(groups):
        lines = []
        for s in range(parts):
            if parts == 1:
                first = (me ^ k) * share
            else:
                source = tile ^ (s // (parts // 2)) ^ (2 * (s % (parts // 2)))
                first = (source * groups + (me ^ k)) * share
            lines.append(plain[pl.ds(pl.multiple_of(first, 8), share)])
        block = jnp.concatenate(lines, axis=0).astype(BF16)
        height = parts * share
        for phase in range(4):
            spread[
                k, phase * height : (phase + 1) * height, phase * width : (phase + 1) * width
            ] = block


def exchange(values, axis, k):
    size = lax.axis_size(axis)
    return lax.ppermute(values, axis, [(i, i ^ k) for i in range(size)])


def body(latent, coarse_filters, mid_filters, fine_filters, coarse_proj, mid_proj):
    groups, tiles = lax.axis_size("grp"), lax.axis_size("tile")
    me, tile = lax.axis_index("grp"), lax.axis_index("tile")
    frames, rows, cols, depth0 = latent.shape
    depth1, depth2 = mid_proj.shape
    width0 = coarse_filters.shape[4]
    height = groups * rows
    cells = height * frames
    own_mid = mid_filters.shape[4]

    early = []
    divided = own_mid % groups == 0 and (own_mid // groups) % 8 == 0
    share, shares = (own_mid // groups, tiles) if divided else (depth1 // groups, 1)
    lanes = 4 * shares * share
    arrived = [exchange(latent, "grp", k) for k in range(1, groups)]
    arrived = [with_layout_constraint(piece, Layout((0, 1, 2, 3))) for piece in arrived]
    pieces = [jnp.transpose(piece, (1, 2, 0, 3)) for piece in [latent] + arrived]

    mid_rows = jnp.transpose(mid_filters, (0, 1, 2, 4, 3))
    if divided:
        mine = call(
            functools.partial(pick_kernel, groups),
            jax.ShapeDtypeStruct((3, 3, 3, share, depth1), BF16),
            [pltpu.VMEM(mid_rows.shape, BF16), pltpu.SemaphoreType.DMA],
            6 * 10**9,
            10**6,
            mid_rows,
            stay=(0,),
        )
        near = [exchange(mine, "tile", k) for k in range(4, tiles, 2)]
        gathered = jnp.stack([mine, *near])
        early = [exchange(gathered, "tile", 1)]
    else:
        every = lax.all_gather(mid_rows, "tile", axis=3, tiled=True)
        mine = lax.dynamic_slice_in_dim(every, me * share, share, axis=3)[None]

    part = call(
        functools.partial(coarse_kernel, groups),
        jax.ShapeDtypeStruct((cols + 2, cells, width0), BF16),
        [pltpu.VMEM((3, height + 2, cols * frames, depth0), BF16)],
        2 * 10**9,
        10**5,
        *pieces,
        coarse_filters,
    )
    straight = call(
        functools.partial(straight_kernel, groups),
        jax.ShapeDtypeStruct((cols, height, frames, depth1), F32),
        [],
        5 * 10**9,
        10**6,
        *pieces,
        coarse_proj,
    )
    parts = [part] + [exchange(part, "grp", k) for k in range(1, groups)]
    if divided:
        later, _ = lax.optimization_barrier((mine, part))
        beyond = exchange(later, "tile", 2)
    odd_out, even_out, own = call(
        functools.partial(project_kernel, groups),
        (
            jax.ShapeDtypeStruct((2, cells, depth1), BF16),
            jax.ShapeDtypeStruct((2, cells, depth1), BF16),
            jax.ShapeDtypeStruct((cols + 2, cells, depth1), BF16),
        ),
        [],
        2 * cells * (cols + 2) * depth0 * depth1,
        2 * 10**6,
        *parts,
        coarse_proj,
        straight,
        *early,
    )
    odd_pairs = [(i, i + 1) for i in range(1, tiles - 1, 2)]
    odd_in = lax.ppermute(odd_out, "tile", odd_pairs + [(j, i) for i, j in odd_pairs])
    even_in = exchange(even_out, "tile", 1)
    if divided:
        gathered, beyond, _ = lax.optimization_barrier((gathered, beyond, own))
        beyond = beyond[None]
        got = early[0]
        mine = jnp.concatenate(
            [gathered[:1], beyond, gathered[1:], got[:1], exchange(beyond, "tile", 1), got[1:]]
        )
    mid_folded = call(
        fold_middle_kernel,
        jax.ShapeDtypeStruct((3, 3, 2, depth1, lanes), BF16),
        [],
        10**6,
        4 * 10**6,
        mine,
    )
    local = (rows + 2) * frames
    *chunks, block = call(
        functools.partial(middle_kernel, groups, rows, frames),
        tuple(
            jax.ShapeDtypeStruct(((cols + 1) * (rows + 1) * frames, lanes), BF16)
            for _ in range(groups)
        )
        + (jax.ShapeDtypeStruct((cols + 2, local, depth1), BF16),),
        [
            pltpu.VMEM((3, cols + 2, cells + 2 * frames, depth1), BF16),
            pltpu.VMEM((3, cols + 2, cells, depth1), BF16),
            pltpu.VMEM((cols + 2, height + 2, frames, depth1), F32),
            pltpu.VMEM((cols + 1, height + 2, frames, lanes), F32),
        ],
        2 * 18 * (cols + 1) * cells * depth1 * lanes,
        5 * 10**6,
        odd_in,
        even_in,
        own,
        mid_folded,
    )
    chunks = [chunks[0]] + [exchange(chunks[k], "grp", k) for k in range(1, groups)]
    fine_folded, spread = call(
        functools.partial(prepare_kernel, groups, shares),
        (
            jax.ShapeDtypeStruct((3, 2, 2, 2 * depth2, 2 * depth2), BF16),
            jax.ShapeDtypeStruct((groups, lanes, 4 * depth2), BF16),
        ),
        [pltpu.VMEM((depth1, depth2), F32)],
        10**6,
        4 * 10**6,
        fine_filters,
        mid_proj,
    )
    tall, broad = 2 * rows, 2 * cols
    return call(
        functools.partial(fine_kernel, groups, frames),
        jax.ShapeDtypeStruct((frames, 2 * tall, 2 * broad, depth2), BF16),
        [
            pltpu.VMEM((3, broad + 2, (tall + 2) * frames, depth2), BF16),
            pltpu.VMEM((3, broad + 2, tall * frames, depth2), BF16),
            pltpu.VMEM((broad + 2, tall, frames, depth2), F32),
        ],
        2 * 24 * (broad + 1) * tall * frames * depth2 * 2 * depth2,
        3 * 10**6,
        *[chunks[k] for k in chunk_order(groups)],
        block,
        spread,
        mid_proj,
        fine_folded,
    )


def solution(mesh):
    in_specs = (
        P(None, "grp", "tile", None),
        P(None, None, None, None, "grp"),
        P(None, None, None, None, "tile"),
        P(),
        P(),
        P(),
    )
    out_specs = P(None, "grp", "tile", None)
    return jax.shard_map(body, mesh=mesh, in_specs=in_specs, out_specs=out_specs, check_vma=False)
```
